32 devices in a mesh: copy: 2 (over x), tm: 2 (over core), space: 8 (over z, y).
Axes of the slice: x: 2, y: 2, z: 4, core: 2. Of those that a mesh axis runs over, the one named last changes fastest.
Arguments:
- initial: float32 [4, 16, 128, 128], P(('copy', 'tm'), 'space'), parts along dimension 0, may hold values from 0.1 to 2
- source: bfloat16 [4, 16, 128, 128], P(('copy', 'tm'), 'space'), parts along dimension 0, may hold values from 0.049804688 to 1
- diffusion: float32 [16, 128, 128], P('space'), may hold values from 0.02 to 0.5
- wind_field: float32 [3, 16, 128, 128], P(None, 'space'), may hold values from -0.6 to 0.6
- buildings: int32 [16, 128, 128], P('space'), may hold values from 0 to 1, as said below
- strength: float32 [2, 4], P('tm'), may hold values from 0.5 to 2
Outputs:
- advanced: float32 [4, 16, 128, 128], P(('copy', 'tm'), 'space'), parts along dimension 0
- final_fine: float32 [4, 16, 128, 128], P(('copy', 'tm'), 'space'), parts along dimension 0
The draws below stay inside these ranges and needn't reach their ends.
There are 2 independent parts, one for each index of `copy`. The reference program is written for one: setup_inputs(seed, part) draws one part's arguments, and reference() takes and returns one part's arrays. A program takes and returns all parts, laid end to end along the dimension named above; an argument that names none is the same for every part. Nothing has to cross between parts.
Inputs may be any that keep to these rules, and one draw needn't show every extreme that they name: buildings stand on the ground as columns.
All inputs are finite; a program needn't handle non-finite values.
Results may differ from the reference program's by a relative error of at most 0.0003.
Values sent between devices are 32-bit elements; how exact they have to be, the bound alone decides.
No kernel may reach another device: no remote copies, remote signals or barrier semaphores. Data moves between devices by JAX's collectives and lax.ppermute only.
A program may use at most 64 MiB of HBM per device.

```python
import math
import jax
import jax.numpy as jnp
from jax import lax

NY = 128
NZ = 128
FINE = 4
NX = 16
BLOCKS = 2


def draw_diffusion(key, part):
    first_key, second_key = jax.random.split(key, 2)
    center = jax.random.uniform(first_key, (), minval=0.0, maxval=1.0)
    places = (jnp.arange(NX, dtype=jnp.float32) + 0.5) / NX
    spread = 0.2
    logs = jax.random.uniform(second_key, (NX, NY, NZ), minval=math.log(0.02), maxval=math.log(0.1))
    base_values = jnp.exp(logs)
    profile = 1.0 + 4.0 * jnp.exp(-((places - center) / spread) ** 2)
    return (base_values * profile[:, None, None]).astype(jnp.float32)


def draw_buildings(key, part):
    first_key, second_key = jax.random.split(key, 2)
    footprint = jax.random.randint(first_key, (NX, NY), 0, 4) == 0
    heights = jax.random.randint(second_key, (NX, NY), 1, NZ // 3 + 1)
    levels = jnp.arange(NZ, dtype=jnp.int32)
    inside = footprint[:, :, None] & (levels[None, None, :] < heights[:, :, None])
    return jnp.where(inside, 1, 0).astype(jnp.int32)


def level_of(stream_key, shape, shards, low, largest):
    def one(dim, parts):
        draws = jax.random.uniform(jax.random.fold_in(jax.random.fold_in(stream_key, 6), dim), (parts,), jnp.float32, low / len(shards), largest / len(shards))
        return jnp.repeat(jnp.exp(draws), shape[dim] // parts).reshape((-1,) + (1,) * (len(shape) - dim - 1))

    factor_of = one(*shards[0])
    for cut in shards[1:]:
        factor_of = factor_of * one(*cut)
    return factor_of


def centred(key, extent, scale, limit, cuts=(), held_as=jnp.bfloat16):
    loudness = level_of(key, extent, cuts, -0.22, 0.18) if cuts else 1.0
    values = jax.random.normal(key, extent, jnp.float32) * scale * loudness
    return jnp.minimum(jnp.maximum(values, -limit), limit).astype(held_as)


def setup_inputs(seed: int = 0, part: int = 0) -> dict:
    arg_keys = jax.random.split(jax.random.key(seed), 7)
    part_splits = jax.random.split(jax.random.fold_in(arg_keys[6], part), 7)
    initial = jnp.clip(jnp.exp(math.log(2.0) - 2.9957323 * jax.random.uniform(part_splits[0], (BLOCKS, NX, NY, NZ), jnp.float32) ** level_of(part_splits[0], (BLOCKS, NX, NY, NZ), ((0, 2), (1, 8)), -0.2, 0.2)), 0.1, 2.0)
    source = jnp.clip(jnp.exp(math.log(1.0) - 2.9996462 * jax.random.uniform(part_splits[1], (BLOCKS, NX, NY, NZ), jnp.float32) ** level_of(part_splits[1], (BLOCKS, NX, NY, NZ), ((0, 2), (1, 8)), -0.2, 0.2)), 0.049804688, 1.0).astype(jnp.bfloat16)
    diffusion = draw_diffusion(jax.random.fold_in(arg_keys[6], 71), part)
    wind_field = centred(arg_keys[3], (3, NX, NY, NZ), 0.15, 0.6, ((1, 8),), jnp.float32)
    buildings = draw_buildings(jax.random.fold_in(arg_keys[6], 71), part)
    strength = jnp.clip(jnp.exp(math.log(2.0) - 1.3862944 * jax.random.uniform(arg_keys[5], (BLOCKS, FINE), jnp.float32) ** level_of(arg_keys[5], (BLOCKS, FINE), ((0, 2),), -0.2, 0.2)), 0.5, 2.0)
    return {"initial": initial, "source": source, "diffusion": diffusion, "wind_field": wind_field, "buildings": buildings, "strength": strength}


lower_bound = 0.5

def ahead(values, direction):
    length = values.shape[direction]
    tail = lax.slice_in_dim(values, 1, length, axis=direction)
    blank = jnp.zeros_like(lax.slice_in_dim(values, 0, 1, axis=direction))
    return jnp.concatenate([tail, blank], axis=direction)

def behind(values, direction):
    length = values.shape[direction]
    head = lax.slice_in_dim(values, 0, length - 1, axis=direction)
    blank = jnp.zeros_like(lax.slice_in_dim(values, 0, 1, axis=direction))
    return jnp.concatenate([blank, head], axis=direction)

def face_terms(masked, winds):
    opened = jnp.where(masked > 0.0, 1.0, 0.0).astype(masked.dtype)
    result = []
    for direction in range(3):
        conduct = jnp.sqrt(masked * ahead(masked, direction))
        velocity = 0.5 * (winds[direction] + ahead(winds[direction], direction)) * opened * ahead(opened, direction)
        result.append((conduct, velocity))
    return tuple(result)

def disk_fields(face_set):
    conduct_sum = jnp.zeros_like(face_set[0][0])
    speed_sum = jnp.zeros_like(face_set[0][0])
    for direction in range(3):
        conduct, velocity = face_set[direction]
        speed = jnp.abs(velocity)
        conduct_sum = conduct_sum + conduct + behind(conduct, direction)
        speed_sum = speed_sum + speed + behind(speed, direction)
    return (conduct_sum, speed_sum)

def operate(values, face_set, rate):
    total = values
    for direction in range(3):
        conduct, velocity = face_set[direction]
        neighbor = ahead(values, direction)
        flowing = conduct * (values - neighbor) + rate * (jnp.maximum(velocity, 0.0) * values + jnp.minimum(velocity, 0.0) * neighbor)
        total = total + flowing - behind(flowing, direction)
    return total

def coefficients(bound):
    theta = (bound + lower_bound) * 0.5
    delta = (bound - lower_bound) * 0.5
    sigma = theta / delta
    rho_one = 1.0 / sigma
    rho_two = 1.0 / (2.0 * sigma - rho_one)
    return (theta, delta, rho_one, rho_two)

def implicit(current, forcing, face_set, rate, bound):
    theta, delta, rho_one, rho_two = coefficients(bound)
    residual = current + forcing - operate(current, face_set, rate)
    update = residual / theta
    moved = current + update
    residual = residual - operate(update, face_set, rate)
    update = rho_two * rho_one * update + 2.0 * rho_two / delta * residual
    return moved + update

def reference(initial, source, diffusion, wind_field, buildings, strength):
    opened = (1 - buildings).astype(jnp.float32)
    masked = diffusion * opened
    forcing = source.astype(jnp.float32) * opened[None]
    face_set = face_terms(masked, (wind_field[0], wind_field[1], wind_field[2]))
    conduct_sum, speed_sum = disk_fields(face_set)
    advanced = []
    bounds = []
    for time_block in range(BLOCKS):
        bound_row = [jnp.max(1.0 + 2.0 * conduct_sum + strength[time_block, fine_step] * speed_sum) for fine_step in range(FINE)]
        bounds.append(bound_row)
        current = initial[time_block] * opened
        for fine_step in range(FINE):
            current = implicit(current, forcing[time_block], face_set, strength[time_block, fine_step], bound_row[fine_step])
        advanced.append(current)
    finals = []
    for time_block in range(BLOCKS):
        if time_block == 0:
            current = initial[0] * opened
        else:
            current = advanced[time_block - 1]
        for fine_step in range(FINE - 1):
            current = implicit(current, forcing[time_block], face_set, strength[time_block, fine_step], bounds[time_block][fine_step])
        finals.append(current)
    return (jnp.stack(advanced), jnp.stack(finals))
```

```python
import functools

import jax
import jax.numpy as jnp
from jax import lax
from jax.experimental import pallas as pl
from jax.experimental.pallas import tpu as pltpu
from jax.sharding import PartitionSpec as P

FINE = 4
LOW = 2 * FINE
lower_bound = 0.5
AXES = ("copy", "tm", "space")
VMEM = pl.BlockSpec(memory_space=pltpu.VMEM)
SMEM = pl.BlockSpec(memory_space=pltpu.SMEM)


def windows(values, place, rows, width):
    total, lanes = values.shape
    start = rows * place - LOW
    first, last = max(start, 0), min(start + width, total)
    parts = []
    if first > start:
        parts.append(jnp.zeros((first - start, lanes), values.dtype))
    parts.append(values[first:last])
    if last < start + width:
        parts.append(jnp.zeros((start + width - last, lanes), values.dtype))
    return jnp.concatenate(parts, axis=0) if len(parts) > 1 else parts[0]


def pack_shared(rows, width, info, diffusion, wind, buildings, out):
    first = info[0] == 0
    for layer in range(diffusion.shape[0]):
        masked = diffusion[layer] * (1 - buildings[layer]).astype(jnp.float32)
        pair = (
            jnp.where(first, masked, wind[1, layer]),
            jnp.where(first, wind[0, layer], wind[2, layer]),
        )
        for field in range(2):
            for place in range(out.shape[0]):
                out[place, field, layer] = windows(pair[field], place, rows, width)


def roll_back(values, axis):
    return pltpu.roll(values, values.shape[axis] - 1, axis)


def face_kernel(rows, width, info, rates, mine, other, initial, source, buildings, *outs):
    faces, packed = outs[:6], outs[6]
    count, layers = mine.shape[0], mine.shape[2]
    total = count * layers
    lanes = mine.shape[-1]
    first = info[0] == 0
    row = lax.broadcasted_iota(jnp.int32, (width, lanes), 0)
    lane = lax.broadcasted_iota(jnp.int32, (width, lanes), 1)
    inner_row = row < width - 1
    inner_lane = lane < lanes - 1
    zero = jnp.zeros((width, lanes), jnp.float32)

    def fields(place):
        spot, layer = place // layers, place % layers
        here = (mine[spot, 0, layer], mine[spot, 1, layer])
        there = (other[spot, 0, layer], other[spot, 1, layer])
        masked = jnp.where(first, here[0], there[0])
        wind_x = jnp.where(first, here[1], there[1])
        wind_y = jnp.where(first, there[0], here[0])
        wind_z = jnp.where(first, there[1], here[1])
        return masked, wind_x, wind_y, wind_z

    def body(place, carry):
        masked, wind_x, wind_y, wind_z, low_conduct, low_speed, peaks = carry
        following = fields(jnp.minimum(place + 1, total - 1))
        inside = place < total - 1
        next_masked = jnp.where(inside, following[0], zero)
        opened = jnp.where(masked > 0.0, 1.0, 0.0)

        def face(masked_ahead, wind_here, wind_ahead, keep):
            conduct = jnp.sqrt(masked * masked_ahead)
            speed = 0.5 * (wind_here + wind_ahead) * opened * jnp.where(masked_ahead > 0.0, 1.0, 0.0)
            if keep is not None:
                conduct, speed = jnp.where(keep, conduct, 0.0), jnp.where(keep, speed, 0.0)
            return conduct, speed

        along_x = face(next_masked, wind_x, following[1], None)
        along_y = face(roll_back(masked, 0), wind_y, roll_back(wind_y, 0), inner_row)
        along_z = face(roll_back(masked, 1), wind_z, roll_back(wind_z, 1), inner_lane)
        for number, value in enumerate(along_x + along_y + along_z):
            faces[number][place] = value
        speeds = [jnp.abs(pair[1]) for pair in (along_x, along_y, along_z)]
        conduct_sum = (
            along_x[0]
            + low_conduct
            + along_y[0]
            + pltpu.roll(along_y[0], 1, 0)
            + along_z[0]
            + pltpu.roll(along_z[0], 1, 1)
        )
        speed_sum = (
            speeds[0]
            + low_speed
            + speeds[1]
            + pltpu.roll(speeds[1], 1, 0)
            + speeds[2]
            + pltpu.roll(speeds[2], 1, 1)
        )
        still = (1.0 + 2.0 * conduct_sum)[LOW : LOW + rows]
        speed_sum = speed_sum[LOW : LOW + rows]
        peaks = tuple(jnp.maximum(peaks[k], still + rates[0, k] * speed_sum) for k in range(FINE))
        return next_masked, *following[1:], along_x[0], speeds[0], peaks

    start = (*fields(0), zero, zero, (jnp.zeros((rows, lanes), jnp.float32),) * FINE)
    peaks = lax.fori_loop(0, total, body, start)[-1]
    bounds = jnp.zeros((8, lanes), jnp.float32)
    place = lax.broadcasted_iota(jnp.int32, (8, lanes), 0)
    for k in range(FINE):
        bounds = jnp.where(place == k, jnp.max(peaks[k]), bounds)
    for layer in range(layers):
        opened = (1 - buildings[layer]).astype(jnp.float32)
        state = initial[0, layer] * opened
        forcing = source[0, layer].astype(jnp.float32) * opened
        for spot in range(count):
            packed[spot, pl.ds(layer * width, width)] = windows(state, spot, rows, width)
            packed[spot, pl.ds((layers + layer) * width, width)] = windows(forcing, spot, rows, width)
    for spot in range(count):
        packed[spot, pl.ds(2 * layers * width, 8)] = bounds


def coefficients(bound):
    theta = (bound + lower_bound) * 0.5
    delta = (bound - lower_bound) * 0.5
    sigma = theta / delta
    rho_one = 1.0 / sigma
    rho_two = 1.0 / (2.0 * sigma - rho_one)
    beta = 2.0 * rho_two / (delta * theta)
    alpha = (1.0 + rho_one * rho_two) / theta + 2.0 * rho_two / delta
    return alpha - beta, beta


def one_step(total, width, layers, state, residual, ahead, faces, packed, rate, near, far):
    lanes = state.shape[-1]
    zero = jnp.zeros((width, lanes), jnp.float32)

    def difference(place, values, values_ahead, low_flow, pairs):
        flow_x = pairs[0] * values + pairs[1] * values_ahead
        flow_y = pairs[2] * values + pairs[3] * roll_back(values, 0)
        flow_z = pairs[4] * values + pairs[5] * roll_back(values, 1)
        change = (flow_x - low_flow) + (flow_y - pltpu.roll(flow_y, 1, 0)) + (flow_z - pltpu.roll(flow_z, 1, 1))
        return change, flow_x

    def first_sweep(place, carry):
        values, low_flow = carry
        values_ahead = state[place + 1]
        pairs = []
        for dim in range(3):
            conduct, speed = faces[2 * dim][place], faces[2 * dim + 1][place]
            pairs.append(conduct + rate * jnp.maximum(speed, 0.0))
            pairs.append(rate * jnp.minimum(speed, 0.0) - conduct)
        for number in range(6):
            ahead[number, place] = pairs[number]
        change, low_flow = difference(place, values, values_ahead, low_flow, pairs)
        spot, layer = place // layers, place % layers
        offset = pl.multiple_of((layers + layer) * width, 8)
        residual[place] = packed[spot, pl.ds(offset, width)] - change
        return values_ahead, low_flow

    def second_sweep(place, carry):
        values, low_flow = carry
        values_ahead = residual[place + 1]
        pairs = [ahead[number, place] for number in range(6)]
        change, low_flow = difference(place, values, values_ahead, low_flow, pairs)
        state[place] = state[place] + (near * values - far * change)
        return values_ahead, low_flow

    lax.fori_loop(0, total, first_sweep, (state[0], zero), unroll=2)
    lax.fori_loop(0, total, second_sweep, (residual[0], zero), unroll=2)


def bounds_of(packed, layers, width):
    bounds = packed[0, pl.ds(2 * layers * width, 8)]
    for spot in range(1, packed.shape[0]):
        bounds = jnp.maximum(bounds, packed[spot, pl.ds(2 * layers * width, 8)])
    return bounds


def first_kernel(rows, width, layers, info, rates, packed, *refs):
    faces, (advanced, third, edge_one, edge_two), (state, residual, ahead) = refs[:6], refs[6:10], refs[10:]
    count = packed.shape[0]
    total = count * layers
    zero = jnp.zeros(state.shape[1:], jnp.float32)
    state[total] = zero
    residual[total] = zero
    for spot in range(count):
        for layer in range(layers):
            state[spot * layers + layer] = packed[spot, pl.ds(layer * width, width)]
    bounds = bounds_of(packed, layers, width)
    for k in range(FINE):
        near, far = coefficients(bounds[k : k + 1])
        one_step(total, width, layers, state, residual, ahead, faces, packed, rates[0, k], near, far)
        if k == FINE - 2:
            third[...] = state[:total, LOW : LOW + rows]
    advanced[...] = state[:total, LOW : LOW + rows]
    edge = min(rows, LOW)
    low, high = state[:total, LOW : LOW + edge], state[:total, LOW + rows - edge : LOW + rows]
    even = info[1] % 2 == 0
    edge_one[...] = jnp.where(even, high, low)
    edge_two[...] = jnp.where(even, low, high)


def second_kernel(rows, width, layers, info, rates, packed, own, halo_one, halo_two, advanced, third, *refs):
    faces, out, (state, residual, ahead) = refs[:6], refs[6], refs[7:]
    total = state.shape[0] - 1
    zero = jnp.zeros(state.shape[1:], jnp.float32)
    state[total] = zero
    residual[total] = zero
    swap = info[2] == 1
    below, above = halo_one[...], halo_two[...]
    low = jnp.where(swap, above, below)
    high = jnp.where(swap, below, above)
    state[:total, :LOW] = jnp.where(info[3] == 1, low, 0.0)
    state[:total, LOW : LOW + rows] = own[...]
    state[:total, LOW + rows : 2 * LOW + rows] = jnp.where(info[4] == 1, high, 0.0)
    if width > 2 * LOW + rows:
        state[:total, 2 * LOW + rows :] = jnp.zeros((total, width - 2 * LOW - rows, state.shape[-1]), jnp.float32)
    bounds = bounds_of(packed, layers, width)
    for k in range(FINE - 1):
        near, far = coefficients(bounds[k : k + 1])
        one_step(total, width, layers, state, residual, ahead, faces, packed, rates[0, k], near, far)
    first = info[0] == 0
    final = jnp.where(first, third[...], state[:total, LOW : LOW + rows])
    shape = out.shape[0:1] + out.shape[2:]
    out[:, 0] = advanced[...].reshape(shape)
    out[:, 1] = final.reshape(shape)


def swapped(array, sizes, partner):
    copies, blocks, count = sizes
    pairs = []
    for c in range(copies):
        for t in range(blocks):
            for s in range(count):
                target = partner(t, s)
                if target is not None:
                    pairs.append(((c * blocks + t) * count + s, (c * blocks + target[0]) * count + target[1]))
    return lax.ppermute(array, AXES, pairs)


def halos(edge_one, edge_two, advanced, sizes, rows, place):
    copies, blocks, count = sizes
    even = place % 2 == 0
    below, above = place > 0, place < count - 1
    if rows >= LOW and blocks == 2 and count % 2 == 0:
        one = swapped(edge_one, sizes, lambda t, s: (1 - t, s ^ 1))
        two = swapped(edge_two, sizes, lambda t, s: (1 - t, ((s + 1) ^ 1) - 1 if 0 < s < count - 1 else s))
        return one, two, even, below, above

    def shifted(values, by):
        return swapped(
            values, sizes, lambda t, s: (t + 1, s + by) if t + 1 < blocks and 0 <= s + by < count else None
        )

    reach = -(-LOW // rows)
    low = jnp.concatenate([shifted(advanced, by) for by in range(reach, 0, -1)], axis=1)[:, -LOW:]
    high = jnp.concatenate([shifted(advanced, -by) for by in range(1, reach + 1)], axis=1)[:, :LOW]
    return low, high, False, True, True


def shards(sizes, initial, source, diffusion, wind_field, buildings, strength):
    copies, blocks, count = sizes
    layers, depth, lanes = diffusion.shape
    total, rows = layers * count, depth // count
    width = -(-(rows + 2 * LOW) // 8) * 8
    block, place = lax.axis_index("tm"), lax.axis_index("space")
    params = pltpu.CompilerParams(vmem_limit_bytes=48 * 1024 * 1024)

    def struct(*shape):
        return jax.ShapeDtypeStruct(shape, jnp.float32)

    half = block % 2
    info = jnp.stack([half, place]).astype(jnp.int32)
    shared = pl.pallas_call(
        functools.partial(pack_shared, rows, width),
        out_shape=struct(count, 2, layers, width, lanes),
        in_specs=[SMEM] + [VMEM] * 3,
        out_specs=VMEM,
        compiler_params=params,
        name="pack_shared",
    )(info, diffusion, wind_field, buildings)
    mine = lax.all_to_all(shared, "space", 0, 0, tiled=True)
    other = swapped(mine, sizes, lambda t, s: (t ^ 1, s))

    out_shape = [struct(total, width, lanes)] * 6 + [struct(count, 2 * layers * width + 8, lanes)]
    *faces, packed = pl.pallas_call(
        functools.partial(face_kernel, rows, width),
        out_shape=out_shape,
        in_specs=[SMEM] * 2 + [VMEM] * 5,
        out_specs=[VMEM] * 7,
        compiler_params=params,
        name="faces",
    )(info, strength, mine, other, initial, source, buildings)
    packed = lax.all_to_all(packed, "space", 0, 0, tiled=True)

    edge = min(rows, LOW)
    scratch = [
        pltpu.VMEM((total + 1, width, lanes), jnp.float32),
        pltpu.VMEM((total + 1, width, lanes), jnp.float32),
        pltpu.VMEM((6, total, width, lanes), jnp.float32),
    ]
    advanced, third, edge_one, edge_two = pl.pallas_call(
        functools.partial(first_kernel, rows, width, layers),
        out_shape=[struct(total, rows, lanes)] * 2 + [struct(total, edge, lanes)] * 2,
        in_specs=[SMEM] * 2 + [VMEM] * 7,
        out_specs=[VMEM] * 4,
        scratch_shapes=scratch,
        compiler_params=params,
        name="four_steps",
    )(info, strength, packed, *faces)

    if blocks == 2:
        own = swapped(advanced, sizes, lambda t, s: (1 - t, s))
    else:
        own = swapped(advanced, sizes, lambda t, s: (t + 1, s) if t + 1 < blocks else None)
    one, two, swap, below, above = halos(edge_one, edge_two, advanced, sizes, rows, place)
    flags = [block, place, swap, below, above]
    info = jnp.stack([jnp.asarray(flag).astype(jnp.int32) for flag in flags])
    result = pl.pallas_call(
        functools.partial(second_kernel, rows, width, layers),
        out_shape=struct(count, 2, layers, rows, lanes),
        in_specs=[SMEM] * 2 + [VMEM] * 12,
        out_specs=VMEM,
        scratch_shapes=scratch,
        compiler_params=params,
        name="three_steps",
    )(info, strength, packed, own, one, two, advanced, third, *faces)
    result = lax.all_to_all(result, "space", 0, 0, tiled=True)
    result = result.transpose(1, 2, 0, 3, 4).reshape(2, 1, layers, depth, lanes)
    return result[0], result[1]


def solution(mesh):
    sizes = tuple(mesh.shape[axis] for axis in AXES)
    in_specs = (
        P(("copy", "tm"), "space", None, None),
        P(("copy", "tm"), "space", None, None),
        P("space", None, None),
        P(None, "space", None, None),
        P("space", None, None),
        P("tm", None),
    )
    out_specs = (P(("copy", "tm"), "space", None, None), P(("copy", "tm"), "space", None, None))
    return jax.shard_map(
        functools.partial(shards, sizes), mesh=mesh, in_specs=in_specs, out_specs=out_specs, check_vma=False
    )
```

```python
import functools

import jax
import jax.numpy as jnp
from jax import lax
from jax.experimental import pallas as pl
from jax.experimental.pallas import tpu as pltpu
from jax.sharding import PartitionSpec as P

FINE = 4
LOW = 2 * FINE
lower_bound = 0.5
AXES = ("copy", "tm", "space")
VMEM = pl.BlockSpec(memory_space=pltpu.VMEM)
SMEM = pl.BlockSpec(memory_space=pltpu.SMEM)


def windows(values, place, rows, width):
    total, lanes = values.shape
    start = rows * place - LOW
    first, last = max(start, 0), min(start + width, total)
    parts = []
    if first > start:
        parts.append(jnp.zeros((first - start, lanes), values.dtype))
    parts.append(values[first:last])
    if last < start + width:
        parts.append(jnp.zeros((start + width - last, lanes), values.dtype))
    return jnp.concatenate(parts, axis=0) if len(parts) > 1 else parts[0]


def pack_shared(rows, width, info, diffusion, wind, buildings, out):
    first = info[0] == 0
    for layer in range(diffusion.shape[0]):
        masked = diffusion[layer] * (1 - buildings[layer]).astype(jnp.float32)
        pair = (
            jnp.where(first, masked, wind[1, layer]),
            jnp.where(first, wind[0, layer], wind[2, layer]),
        )
        for field in range(2):
            for place in range(out.shape[0]):
                out[place, field, layer] = windows(pair[field], place, rows, width)


def roll_back(values, axis):
    return pltpu.roll(values, values.shape[axis] - 1, axis)


def face_kernel(rows, width, info, rates, mine, other, initial, source, buildings, *outs):
    faces, packed = outs[:6], outs[6]
    count, layers = mine.shape[0], mine.shape[2]
    total = count * layers
    lanes = mine.shape[-1]
    first = info[0] == 0
    row = lax.broadcasted_iota(jnp.int32, (width, lanes), 0)
    lane = lax.broadcasted_iota(jnp.int32, (width, lanes), 1)
    inner_row = row < width - 1
    inner_lane = lane < lanes - 1
    zero = jnp.zeros((width, lanes), jnp.float32)

    def fields(place):
        spot, layer = place // layers, place % layers
        here = (mine[spot, 0, layer], mine[spot, 1, layer])
        there = (other[spot, 0, layer], other[spot, 1, layer])
        masked = jnp.where(first, here[0], there[0])
        wind_x = jnp.where(first, here[1], there[1])
        wind_y = jnp.where(first, there[0], here[0])
        wind_z = jnp.where(first, there[1], here[1])
        return masked, wind_x, wind_y, wind_z

    def body(place, carry):
        masked, wind_x, wind_y, wind_z, low_conduct, low_speed, peaks = carry
        following = fields(jnp.minimum(place + 1, total - 1))
        inside = place < total - 1
        next_masked = jnp.where(inside, following[0], zero)
        opened = jnp.where(masked > 0.0, 1.0, 0.0)

        def face(masked_ahead, wind_here, wind_ahead, keep):
            conduct = jnp.sqrt(masked * masked_ahead)
            speed = 0.5 * (wind_here + wind_ahead) * opened * jnp.where(masked_ahead > 0.0, 1.0, 0.0)
            if keep is not None:
                conduct, speed = jnp.where(keep, conduct, 0.0), jnp.where(keep, speed, 0.0)
            return conduct, speed

        along_x = face(next_masked, wind_x, following[1], None)
        along_y = face(roll_back(masked, 0), wind_y, roll_back(wind_y, 0), inner_row)
        along_z = face(roll_back(masked, 1), wind_z, roll_back(wind_z, 1), inner_lane)
        for number, value in enumerate(along_x + along_y + along_z):
            faces[number][place] = value
        speeds = [jnp.abs(pair[1]) for pair in (along_x, along_y, along_z)]
        conduct_sum = (
            along_x[0]
            + low_conduct
            + along_y[0]
            + pltpu.roll(along_y[0], 1, 0)
            + along_z[0]
            + pltpu.roll(along_z[0], 1, 1)
        )
        speed_sum = (
            speeds[0]
            + low_speed
            + speeds[1]
            + pltpu.roll(speeds[1], 1, 0)
            + speeds[2]
            + pltpu.roll(speeds[2], 1, 1)
        )
        still = (1.0 + 2.0 * conduct_sum)[LOW : LOW + rows]
        speed_sum = speed_sum[LOW : LOW + rows]
        peaks = tuple(jnp.maximum(peaks[k], still + rates[0, k] * speed_sum) for k in range(FINE))
        return next_masked, *following[1:], along_x[0], speeds[0], peaks

    start = (*fields(0), zero, zero, (jnp.zeros((rows, lanes), jnp.float32),) * FINE)
    peaks = lax.fori_loop(0, total, body, start, unroll=8)[-1]
    bounds = jnp.zeros((8, lanes), jnp.float32)
    place = lax.broadcasted_iota(jnp.int32, (8, lanes), 0)
    for k in range(FINE):
        bounds = jnp.where(place == k, jnp.max(peaks[k]), bounds)
    for layer in range(layers):
        opened = (1 - buildings[layer]).astype(jnp.float32)
        state = initial[0, layer] * opened
        forcing = source[0, layer].astype(jnp.float32) * opened
        for spot in range(count):
            packed[spot, pl.ds(layer * width, width)] = windows(state, spot, rows, width)
            packed[spot, pl.ds((layers + layer) * width, width)] = windows(forcing, spot, rows, width)
    for spot in range(count):
        packed[spot, pl.ds(2 * layers * width, 8)] = bounds


def coefficients(bound):
    theta = (bound + lower_bound) * 0.5
    delta = (bound - lower_bound) * 0.5
    sigma = theta / delta
    rho_one = 1.0 / sigma
    rho_two = 1.0 / (2.0 * sigma - rho_one)
    beta = 2.0 * rho_two / (delta * theta)
    alpha = (1.0 + rho_one * rho_two) / theta + 2.0 * rho_two / delta
    return alpha - beta, beta


def one_step(total, width, layers, state, residual, ahead, faces, packed, rate, near, far):
    lanes = state.shape[-1]
    zero = jnp.zeros((width, lanes), jnp.float32)

    def difference(place, values, values_ahead, low_flow, pairs):
        flow_x = pairs[0] * values + pairs[1] * values_ahead
        flow_y = pairs[2] * values + pairs[3] * roll_back(values, 0)
        flow_z = pairs[4] * values + pairs[5] * roll_back(values, 1)
        change = (flow_x - low_flow) + (flow_y - pltpu.roll(flow_y, 1, 0)) + (flow_z - pltpu.roll(flow_z, 1, 1))
        return change, flow_x

    def first_sweep(place, carry):
        values, low_flow = carry
        values_ahead = state[place + 1]
        pairs = []
        for dim in range(3):
            conduct, speed = faces[2 * dim][place], faces[2 * dim + 1][place]
            pairs.append(conduct + rate * jnp.maximum(speed, 0.0))
            pairs.append(rate * jnp.minimum(speed, 0.0) - conduct)
        for number in range(6):
            ahead[number, place] = pairs[number]
        change, low_flow = difference(place, values, values_ahead, low_flow, pairs)
        spot, layer = place // layers, place % layers
        offset = pl.multiple_of((layers + layer) * width, 8)
        residual[place] = packed[spot, pl.ds(offset, width)] - change
        return values_ahead, low_flow

    def second_sweep(place, carry):
        values, low_flow = carry
        values_ahead = residual[place + 1]
        pairs = [ahead[number, place] for number in range(6)]
        change, low_flow = difference(place, values, values_ahead, low_flow, pairs)
        state[place] = state[place] + (near * values - far * change)
        return values_ahead, low_flow

    lax.fori_loop(0, total, first_sweep, (state[0], zero), unroll=8)
    lax.fori_loop(0, total, second_sweep, (residual[0], zero), unroll=8)


def bounds_of(packed, layers, width):
    bounds = packed[0, pl.ds(2 * layers * width, 8)]
    for spot in range(1, packed.shape[0]):
        bounds = jnp.maximum(bounds, packed[spot, pl.ds(2 * layers * width, 8)])
    return bounds


def first_kernel(rows, width, layers, info, rates, packed, *refs):
    faces, (advanced, third, edge_one, edge_two), (state, residual, ahead) = refs[:6], refs[6:10], refs[10:]
    count = packed.shape[0]
    total = count * layers
    zero = jnp.zeros(state.shape[1:], jnp.float32)
    state[total] = zero
    residual[total] = zero
    for spot in range(count):
        for layer in range(layers):
            state[spot * layers + layer] = packed[spot, pl.ds(layer * width, width)]
    bounds = bounds_of(packed, layers, width)
    for k in range(FINE):
        near, far = coefficients(bounds[k : k + 1])
        one_step(total, width, layers, state, residual, ahead, faces, packed, rates[0, k], near, far)
        if k == FINE - 2:
            third[...] = state[:total, LOW : LOW + rows]
    advanced[...] = state[:total, LOW : LOW + rows]
    edge = min(rows, LOW)
    low, high = state[:total, LOW : LOW + edge], state[:total, LOW + rows - edge : LOW + rows]
    even = info[1] % 2 == 0
    edge_one[...] = jnp.where(even, high, low)
    edge_two[...] = jnp.where(even, low, high)


def second_kernel(rows, width, layers, info, rates, packed, own, halo_one, halo_two, advanced, third, *refs):
    faces, out, (state, residual, ahead) = refs[:6], refs[6], refs[7:]
    total = state.shape[0] - 1
    zero = jnp.zeros(state.shape[1:], jnp.float32)
    state[total] = zero
    residual[total] = zero
    swap = info[2] == 1
    below, above = halo_one[...], halo_two[...]
    low = jnp.where(swap, above, below)
    high = jnp.where(swap, below, above)
    state[:total, :LOW] = jnp.where(info[3] == 1, low, 0.0)
    state[:total, LOW : LOW + rows] = own[...]
    state[:total, LOW + rows : 2 * LOW + rows] = jnp.where(info[4] == 1, high, 0.0)
    if width > 2 * LOW + rows:
        state[:total, 2 * LOW + rows :] = jnp.zeros((total, width - 2 * LOW - rows, state.shape[-1]), jnp.float32)
    bounds = bounds_of(packed, layers, width)
    for k in range(FINE - 1):
        near, far = coefficients(bounds[k : k + 1])
        one_step(total, width, layers, state, residual, ahead, faces, packed, rates[0, k], near, far)
    first = info[0] == 0
    final = jnp.where(first, third[...], state[:total, LOW : LOW + rows])
    shape = out.shape[0:1] + out.shape[2:]
    out[:, 0] = advanced[...].reshape(shape)
    out[:, 1] = final.reshape(shape)


def swapped(array, sizes, partner):
    copies, blocks, count = sizes
    pairs = []
    for c in range(copies):
        for t in range(blocks):
            for s in range(count):
                target = partner(t, s)
                if target is not None:
                    pairs.append(((c * blocks + t) * count + s, (c * blocks + target[0]) * count + target[1]))
    return lax.ppermute(array, AXES, pairs)


def halos(edge_one, edge_two, advanced, sizes, rows, place):
    copies, blocks, count = sizes
    even = place % 2 == 0
    below, above = place > 0, place < count - 1
    if rows >= LOW and blocks == 2 and count % 2 == 0:
        one = swapped(edge_one, sizes, lambda t, s: (1 - t, s ^ 1))
        two = swapped(edge_two, sizes, lambda t, s: (1 - t, ((s + 1) ^ 1) - 1 if 0 < s < count - 1 else s))
        return one, two, even, below, above

    def shifted(values, by):
        return swapped(
            values, sizes, lambda t, s: (t + 1, s + by) if t + 1 < blocks and 0 <= s + by < count else None
        )

    reach = -(-LOW // rows)
    low = jnp.concatenate([shifted(advanced, by) for by in range(reach, 0, -1)], axis=1)[:, -LOW:]
    high = jnp.concatenate([shifted(advanced, -by) for by in range(1, reach + 1)], axis=1)[:, :LOW]
    return low, high, False, True, True


def shards(sizes, initial, source, diffusion, wind_field, buildings, strength):
    copies, blocks, count = sizes
    layers, depth, lanes = diffusion.shape
    total, rows = layers * count, depth // count
    width = -(-(rows + 2 * LOW) // 8) * 8
    block, place = lax.axis_index("tm"), lax.axis_index("space")
    params = pltpu.CompilerParams(vmem_limit_bytes=48 * 1024 * 1024)

    def struct(*shape):
        return jax.ShapeDtypeStruct(shape, jnp.float32)

    half = block % 2
    info = jnp.stack([half, place]).astype(jnp.int32)
    shared = pl.pallas_call(
        functools.partial(pack_shared, rows, width),
        out_shape=struct(count, 2, layers, width, lanes),
        in_specs=[SMEM] + [VMEM] * 3,
        out_specs=VMEM,
        compiler_params=params,
        name="pack_shared",
    )(info, diffusion, wind_field, buildings)
    mine = lax.all_to_all(shared, "space", 0, 0, tiled=True)
    other = swapped(mine, sizes, lambda t, s: (t ^ 1, s))

    out_shape = [struct(total, width, lanes)] * 6 + [struct(count, 2 * layers * width + 8, lanes)]
    *faces, packed = pl.pallas_call(
        functools.partial(face_kernel, rows, width),
        out_shape=out_shape,
        in_specs=[SMEM] * 2 + [VMEM] * 5,
        out_specs=[VMEM] * 7,
        compiler_params=params,
        name="faces",
    )(info, strength, mine, other, initial, source, buildings)
    packed = lax.all_to_all(packed, "space", 0, 0, tiled=True)

    edge = min(rows, LOW)
    scratch = [
        pltpu.VMEM((total + 1, width, lanes), jnp.float32),
        pltpu.VMEM((total + 1, width, lanes), jnp.float32),
        pltpu.VMEM((6, total, width, lanes), jnp.float32),
    ]
    advanced, third, edge_one, edge_two = pl.pallas_call(
        functools.partial(first_kernel, rows, width, layers),
        out_shape=[struct(total, rows, lanes)] * 2 + [struct(total, edge, lanes)] * 2,
        in_specs=[SMEM] * 2 + [VMEM] * 7,
        out_specs=[VMEM] * 4,
        scratch_shapes=scratch,
        compiler_params=params,
        name="four_steps",
    )(info, strength, packed, *faces)

    if blocks == 2:
        own = swapped(advanced, sizes, lambda t, s: (1 - t, s))
    else:
        own = swapped(advanced, sizes, lambda t, s: (t + 1, s) if t + 1 < blocks else None)
    one, two, swap, below, above = halos(edge_one, edge_two, advanced, sizes, rows, place)
    flags = [block, place, swap, below, above]
    info = jnp.stack([jnp.asarray(flag).astype(jnp.int32) for flag in flags])
    result = pl.pallas_call(
        functools.partial(second_kernel, rows, width, layers),
        out_shape=struct(count, 2, layers, rows, lanes),
        in_specs=[SMEM] * 2 + [VMEM] * 12,
        out_specs=VMEM,
        scratch_shapes=scratch,
        compiler_params=params,
        name="three_steps",
    )(info, strength, packed, own, one, two, advanced, third, *faces)
    result = lax.all_to_all(result, "space", 0, 0, tiled=True)
    result = result.transpose(1, 2, 0, 3, 4).reshape(2, 1, layers, depth, lanes)
    return result[0], result[1]


def solution(mesh):
    sizes = tuple(mesh.shape[axis] for axis in AXES)
    in_specs = (
        P(("copy", "tm"), "space", None, None),
        P(("copy", "tm"), "space", None, None),
        P("space", None, None),
        P(None, "space", None, None),
        P("space", None, None),
        P("tm", None),
    )
    out_specs = (P(("copy", "tm"), "space", None, None), P(("copy", "tm"), "space", None, None))
    return jax.shard_map(
        functools.partial(shards, sizes), mesh=mesh, in_specs=in_specs, out_specs=out_specs, check_vma=False
    )
```

```python
import functools

import jax
import jax.numpy as jnp
from jax import lax
from jax.experimental import pallas as pl
from jax.experimental.pallas import tpu as pltpu
from jax.sharding import PartitionSpec as P

FINE = 4
LOW = 2 * FINE
lower_bound = 0.5
AXES = ("copy", "tm", "space")
VMEM = pl.BlockSpec(memory_space=pltpu.VMEM)
SMEM = pl.BlockSpec(memory_space=pltpu.SMEM)


def windows(values, place, rows, width):
    total, lanes = values.shape
    start = rows * place - LOW
    first, last = max(start, 0), min(start + width, total)
    parts = []
    if first > start:
        parts.append(jnp.zeros((first - start, lanes), values.dtype))
    parts.append(values[first:last])
    if last < start + width:
        parts.append(jnp.zeros((start + width - last, lanes), values.dtype))
    return jnp.concatenate(parts, axis=0) if len(parts) > 1 else parts[0]


def load_kernel(info, initial, source, diffusion, wind, buildings, masked, winds, state, forcing, edge_one, edge_two, *rest):
    fresh, early, late, solid, sems = rest
    pairs = ((diffusion, fresh), (buildings, solid), (wind, winds), (initial.at[0], early), (source.at[0], late))
    copies = [pltpu.make_async_copy(*pair, sems.at[number]) for number, pair in enumerate(pairs)]
    for copy in copies:
        copy.start()
    for copy in copies[:3]:
        copy.wait()
    opened = (1 - solid[...]).astype(jnp.float32)
    masked[...] = fresh[...] * opened
    first, even = info[0] == 0, info[1] % 2 == 0
    last = masked.shape[0] - 1
    low = jnp.where(first, masked[0], winds[0, 0])
    high = jnp.where(first, masked[last], winds[0, last])
    edge_one[...] = jnp.where(even, high, low)
    edge_two[...] = jnp.where(even, low, high)
    for copy in copies[3:]:
        copy.wait()
    state[...] = early[...] * opened
    forcing[...] = late[...].astype(jnp.float32) * opened


def pack_shared(rows, width, info, masked, wind, same, across):
    first, spot = info[0] == 0, info[1]
    half = same.shape[0]
    for layer in range(masked.shape[0]):
        pair = (
            jnp.where(first, masked[layer], wind[1, layer]),
            jnp.where(first, wind[0, layer], wind[2, layer]),
        )
        for field in range(2):
            for place in range(half):
                even = windows(pair[field], 2 * place, rows, width)
                odd = windows(pair[field], 2 * place + 1, rows, width)
                swap = spot % 2 == 1
                same[place ^ (spot // 2), field, layer] = jnp.where(swap, odd, even)
                across[place ^ (spot // 2), field, layer] = jnp.where(swap, even, odd)


def pack_own(rows, width, state, forcing, packed):
    layers = state.shape[0]
    for layer in range(layers):
        for spot in range(packed.shape[0]):
            packed[spot, pl.ds(layer * width, width)] = windows(state[layer], spot, rows, width)
            packed[spot, pl.ds((layers + layer) * width, width)] = windows(forcing[layer], spot, rows, width)


def bound_kernel(rows, width, info, rates, mine, other, masked, wind, state, forcing, out):
    first, even = info[0] == 0, info[1] % 2 == 0
    here, there = (mine[0], mine[1]), (other[0], other[1])

    def sides(one, two, keep):
        above, below = jnp.where(even, one, two), jnp.where(even, two, one)
        if keep:
            below, above = jnp.where(info[2] == 1, below, 0.0), jnp.where(info[3] == 1, above, 0.0)
        return below, above

    masked_sides = sides(jnp.where(first, here[0], there[0]), jnp.where(first, here[1], there[1]), True)
    wind_sides = sides(jnp.where(first, there[0], here[0]), jnp.where(first, there[1], here[1]), False)
    layers, depth, lanes = masked.shape
    chunk = 32 if depth % 32 == 0 else depth
    row = lax.broadcasted_iota(jnp.int32, (chunk, lanes), 0)
    inner_lane = lax.broadcasted_iota(jnp.int32, (chunk, lanes), 1) < lanes - 1

    def face(here, ahead, wind_here, wind_ahead):
        both = jnp.where((here > 0.0) & (ahead > 0.0), 1.0, 0.0)
        return jnp.sqrt(here * ahead), jnp.abs(0.5 * (wind_here + wind_ahead) * both)

    peaks = [jnp.zeros((chunk, lanes), jnp.float32)] * FINE
    edge = [[jnp.zeros((1, lanes), jnp.float32)] * 2 for _ in range(layers)]
    for start in range(0, depth, chunk):
        part = pl.ds(start, chunk)
        fields = [masked_sides[0][start : start + chunk]]
        fields += [masked[layer, part] for layer in range(layers)]
        fields += [masked_sides[1][start : start + chunk]]
        winds = [wind_sides[0][start : start + chunk]]
        winds += [wind[0, layer, part] for layer in range(layers)]
        winds += [wind_sides[1][start : start + chunk]]
        below = face(fields[0], fields[1], winds[0], winds[1])
        for layer in range(layers):
            field = fields[layer + 1]
            above = face(field, fields[layer + 2], winds[layer + 1], winds[layer + 2])
            sums = [above[0] + below[0], above[1] + below[1]]
            below = above
            flow = wind[1, layer, part]
            if start + chunk < depth:
                following = pl.ds(start + 1, chunk)
                pair = face(field, masked[layer, following], flow, wind[1, layer, following])
            else:
                pair = face(field, roll_back(field, 0), flow, roll_back(flow, 0))
                pair = [jnp.where(row < chunk - 1, value, 0.0) for value in pair]
            for number in range(2):
                value = pair[number]
                lower = jnp.where(row == 0, edge[layer][number], pltpu.roll(value, 1, 0))
                edge[layer][number] = value[chunk - 1 : chunk]
                sums[number] = sums[number] + value + lower
            flow = wind[2, layer, part]
            pair = face(field, roll_back(field, 1), flow, roll_back(flow, 1))
            for number in range(2):
                value = jnp.where(inner_lane, pair[number], 0.0)
                sums[number] = sums[number] + value + pltpu.roll(value, 1, 1)
            still = 1.0 + 2.0 * sums[0]
            for k in range(FINE):
                peaks[k] = jnp.maximum(peaks[k], still + rates[0, k] * sums[1])
    bounds = jnp.zeros((8, lanes), jnp.float32)
    place = lax.broadcasted_iota(jnp.int32, (8, lanes), 0)
    for k in range(FINE):
        bounds = jnp.where(place == k, jnp.max(peaks[k]), bounds)
    pack_own(rows, width, state, forcing, out)
    start = out.shape[1] - 8
    for spot in range(out.shape[0]):
        out[spot, pl.ds(start, 8)] = bounds


def roll_back(values, axis):
    return pltpu.roll(values, values.shape[axis] - 1, axis)


def face_kernel(info, mine, other, *faces):
    count, layers, width, lanes = mine.shape[0], *mine.shape[2:]
    total = count * layers
    first, own = info[0] == 0, info[1]
    row = lax.broadcasted_iota(jnp.int32, (width, lanes), 0)
    lane = lax.broadcasted_iota(jnp.int32, (width, lanes), 1)
    inner_row = row < width - 1
    inner_lane = lane < lanes - 1
    zero = jnp.zeros((width, lanes), jnp.float32)

    def fields(place):
        spot, layer = (place // layers) ^ own, place % layers
        here = (mine[spot, 0, layer], mine[spot, 1, layer])
        there = (other[spot, 0, layer], other[spot, 1, layer])
        masked = jnp.where(first, here[0], there[0])
        wind_x = jnp.where(first, here[1], there[1])
        wind_y = jnp.where(first, there[0], here[0])
        wind_z = jnp.where(first, there[1], here[1])
        return masked, wind_x, wind_y, wind_z

    def body(place, carry):
        masked, wind_x, wind_y, wind_z = carry
        following = fields(jnp.minimum(place + 1, total - 1))
        next_masked = jnp.where(place < total - 1, following[0], zero)
        opened = jnp.where(masked > 0.0, 1.0, 0.0)

        def face(masked_ahead, wind_here, wind_ahead, keep):
            conduct = jnp.sqrt(masked * masked_ahead)
            speed = 0.5 * (wind_here + wind_ahead) * opened * jnp.where(masked_ahead > 0.0, 1.0, 0.0)
            if keep is not None:
                conduct, speed = jnp.where(keep, conduct, 0.0), jnp.where(keep, speed, 0.0)
            return conduct, speed

        along_x = face(next_masked, wind_x, following[1], None)
        along_y = face(roll_back(masked, 0), wind_y, roll_back(wind_y, 0), inner_row)
        along_z = face(roll_back(masked, 1), wind_z, roll_back(wind_z, 1), inner_lane)
        for number, value in enumerate(along_x + along_y + along_z):
            faces[number][place] = value
        return next_masked, *following[1:]

    lax.fori_loop(0, total, body, fields(0), unroll=8)


def coefficients(bound):
    theta = (bound + lower_bound) * 0.5
    delta = (bound - lower_bound) * 0.5
    sigma = theta / delta
    rho_one = 1.0 / sigma
    rho_two = 1.0 / (2.0 * sigma - rho_one)
    beta = 2.0 * rho_two / (delta * theta)
    alpha = (1.0 + rho_one * rho_two) / theta + 2.0 * rho_two / delta
    return alpha - beta, beta


def one_step(total, width, layers, state, residual, ahead, faces, packed, rate, near, far):
    lanes = state.shape[-1]
    zero = jnp.zeros((width, lanes), jnp.float32)

    def difference(place, values, values_ahead, low_flow, pairs):
        flow_x = pairs[0] * values + pairs[1] * values_ahead
        flow_y = pairs[2] * values + pairs[3] * roll_back(values, 0)
        flow_z = pairs[4] * values + pairs[5] * roll_back(values, 1)
        change = (flow_x - low_flow) + (flow_y - pltpu.roll(flow_y, 1, 0)) + (flow_z - pltpu.roll(flow_z, 1, 1))
        return change, flow_x

    def first_sweep(place, carry):
        values, low_flow = carry
        values_ahead = state[place + 1]
        pairs = []
        for dim in range(3):
            conduct, speed = faces[2 * dim][place], faces[2 * dim + 1][place]
            pairs.append(conduct + rate * jnp.maximum(speed, 0.0))
            pairs.append(rate * jnp.minimum(speed, 0.0) - conduct)
        for number in range(6):
            ahead[number, place] = pairs[number]
        change, low_flow = difference(place, values, values_ahead, low_flow, pairs)
        spot, layer = place // layers, place % layers
        offset = pl.multiple_of((layers + layer) * width, 8)
        residual[place] = packed[spot, pl.ds(offset, width)] - change
        return values_ahead, low_flow

    def second_sweep(place, carry):
        values, low_flow = carry
        values_ahead = residual[place + 1]
        pairs = [ahead[number, place] for number in range(6)]
        change, low_flow = difference(place, values, values_ahead, low_flow, pairs)
        state[place] = state[place] + (near * values - far * change)
        return values_ahead, low_flow

    lax.fori_loop(0, total, first_sweep, (state[0], zero), unroll=8)
    lax.fori_loop(0, total, second_sweep, (residual[0], zero), unroll=8)


def bounds_of(packed):
    part = pl.ds(packed.shape[1] - 8, 8)
    bounds = packed[0, part]
    for entry in range(1, packed.shape[0]):
        bounds = jnp.maximum(bounds, packed[entry, part])
    return bounds


def first_kernel(rows, width, layers, info, rates, packed, *refs):
    faces, (advanced, third, edge_one, edge_two), (state, residual, ahead) = refs[:6], refs[6:10], refs[10:]
    total = state.shape[0] - 1
    zero = jnp.zeros(state.shape[1:], jnp.float32)
    state[total] = zero
    residual[total] = zero
    for place in range(total):
        state[place] = packed[place // layers, pl.ds(place % layers * width, width)]
    bounds = bounds_of(packed)
    for k in range(FINE):
        near, far = coefficients(bounds[k : k + 1])
        one_step(total, width, layers, state, residual, ahead, faces, packed, rates[0, k], near, far)
        if k == FINE - 2:
            third[...] = state[:total, LOW : LOW + rows]
    advanced[...] = state[:total, LOW : LOW + rows]
    edge = min(rows, LOW)
    low, high = state[:total, LOW : LOW + edge], state[:total, LOW + rows - edge : LOW + rows]
    even = info[1] % 2 == 0
    edge_one[...] = jnp.where(even, high, low)
    edge_two[...] = jnp.where(even, low, high)


def second_kernel(rows, width, layers, info, rates, packed, passed, halo_one, halo_two, advanced, third, *refs):
    faces, out, (state, residual, ahead) = refs[:6], refs[6], refs[7:]
    total = state.shape[0] - 1
    zero = jnp.zeros(state.shape[1:], jnp.float32)
    state[total] = zero
    residual[total] = zero
    swap = info[2] == 1
    below, above = halo_one[...], halo_two[...]
    low = jnp.where(swap, above, below)
    high = jnp.where(swap, below, above)
    state[:total, :LOW] = jnp.where(info[3] == 1, low, 0.0)
    state[:total, LOW : LOW + rows] = passed[...]
    state[:total, LOW + rows : 2 * LOW + rows] = jnp.where(info[4] == 1, high, 0.0)
    if width > 2 * LOW + rows:
        state[:total, 2 * LOW + rows :] = jnp.zeros((total, width - 2 * LOW - rows, state.shape[-1]), jnp.float32)
    bounds = bounds_of(packed)
    for k in range(FINE - 1):
        near, far = coefficients(bounds[k : k + 1])
        one_step(total, width, layers, state, residual, ahead, faces, packed, rates[0, k], near, far)
    first = info[0] == 0
    final = jnp.where(first, third[...], state[:total, LOW : LOW + rows])
    shape = out.shape[0:1] + out.shape[2:]
    out[:, 0] = advanced[...].reshape(shape)
    out[:, 1] = final.reshape(shape)


def swapped(array, sizes, partner):
    copies, blocks, count = sizes
    pairs = []
    for c in range(copies):
        for t in range(blocks):
            for s in range(count):
                target = partner(t, s)
                if target is not None:
                    pairs.append(((c * blocks + t) * count + s, (c * blocks + target[0]) * count + target[1]))
    return lax.ppermute(array, AXES, pairs)


def outer_partner(count):
    return lambda t, s: (t, ((s + 1) ^ 1) - 1) if 0 < s < count - 1 else (t ^ 1, s)


def halos(edge_one, edge_two, advanced, sizes, rows, place):
    copies, blocks, count = sizes
    even = place % 2 == 0
    below, above = place > 0, place < count - 1
    if rows >= LOW and blocks == 2 and count % 2 == 0:
        one = swapped(edge_one, sizes, lambda t, s: (1 - t, s ^ 1))
        two = swapped(edge_two, sizes, lambda t, s: (1 - t, ((s + 1) ^ 1) - 1 if 0 < s < count - 1 else s))
        return one, two, even, below, above

    def shifted(values, by):
        return swapped(
            values, sizes, lambda t, s: (t + 1, s + by) if t + 1 < blocks and 0 <= s + by < count else None
        )

    reach = -(-LOW // rows)
    low = jnp.concatenate([shifted(advanced, by) for by in range(reach, 0, -1)], axis=1)[:, -LOW:]
    high = jnp.concatenate([shifted(advanced, -by) for by in range(1, reach + 1)], axis=1)[:, :LOW]
    return low, high, False, True, True


def shards(sizes, initial, source, diffusion, wind_field, buildings, strength):
    copies, blocks, count = sizes
    layers, depth, lanes = diffusion.shape
    total, rows = layers * count, depth // count
    width = -(-(rows + 2 * LOW) // 8) * 8
    block, place = lax.axis_index("tm"), lax.axis_index("space")
    params = pltpu.CompilerParams(vmem_limit_bytes=48 * 1024 * 1024)

    def struct(*shape):
        return jax.ShapeDtypeStruct(shape, jnp.float32)

    def call(kernel, outs, in_specs, name, *operands, **options):
        return pl.pallas_call(
            kernel,
            out_shape=outs,
            in_specs=in_specs,
            out_specs=[VMEM] * len(outs),
            name=name,
            **{"compiler_params": params, **options},
        )(*operands)

    half = block % 2
    flags = [half, place, place > 0, place < count - 1]
    info = jnp.stack([jnp.asarray(flag).astype(jnp.int32) for flag in flags])
    slab = struct(layers, depth, lanes)
    outer = struct(depth, lanes)
    hold = pltpu.VMEM((layers, depth, lanes), jnp.float32)
    anywhere = pl.BlockSpec(memory_space=pltpu.HBM)
    arrays = (initial, source, diffusion, wind_field, buildings)
    masked, winds, state, forcing, edge_one, edge_two = call(
        load_kernel,
        [slab, struct(3, layers, depth, lanes), slab, slab, outer, outer],
        [SMEM] + [anywhere] * 5,
        "load",
        info,
        *(pltpu.with_memory_space_constraint(array, pltpu.HBM) for array in arrays),
        scratch_shapes=[
            hold,
            hold,
            pltpu.VMEM((layers, depth, lanes), source.dtype),
            pltpu.VMEM((layers, depth, lanes), jnp.int32),
            pltpu.SemaphoreType.DMA((5,)),
        ],
    )
    edge_one = swapped(edge_one, sizes, lambda t, s: (t, s ^ 1))
    edge_two = swapped(edge_two, sizes, outer_partner(count))
    same, across = call(
        functools.partial(pack_shared, rows, width),
        [struct(count // 2, 2, layers, width, lanes)] * 2,
        [SMEM] + [VMEM] * 2,
        "pack_shared",
        info,
        masked,
        winds,
    )
    across = swapped(across, sizes, lambda t, s: (t, s ^ 1))
    even = [swapped(same[step], sizes, lambda t, s: (t, s ^ (2 * step))) for step in range(1, count // 2)]
    across, *even = lax.optimization_barrier((across, *even))
    edges = jnp.stack([edge_one, edge_two])
    other_edges = swapped(edges, sizes, lambda t, s: (t ^ 1, s))
    (packed,) = call(
        functools.partial(bound_kernel, rows, width),
        [struct(count, 2 * layers * width + 8, lanes)],
        [SMEM] * 2 + [VMEM] * 6,
        "bounds",
        info,
        strength,
        edges,
        other_edges,
        masked,
        winds,
        state,
        forcing,
    )
    odd = [swapped(across[step], sizes, lambda t, s: (t, s ^ (2 * step))) for step in range(1, count // 2)]
    parts = [part for pair in zip([same[0], *even], [across[0], *odd]) for part in pair]
    *parts, _ = lax.optimization_barrier((*parts, packed))
    packed = lax.all_to_all(packed, "space", 0, 0, tiled=True)
    mine = jnp.stack(parts)
    other = swapped(mine, sizes, lambda t, s: (t ^ 1, s))
    faces = call(face_kernel, [struct(total, width, lanes)] * 6, [SMEM] + [VMEM] * 2, "faces", info, mine, other)

    edge = min(rows, LOW)
    scratch = [
        pltpu.VMEM((total + 1, width, lanes), jnp.float32),
        pltpu.VMEM((total + 1, width, lanes), jnp.float32),
        pltpu.VMEM((6, total, width, lanes), jnp.float32),
    ]
    advanced, third, edge_one, edge_two = pl.pallas_call(
        functools.partial(first_kernel, rows, width, layers),
        out_shape=[struct(total, rows, lanes)] * 2 + [struct(total, edge, lanes)] * 2,
        in_specs=[SMEM] * 2 + [VMEM] * 7,
        out_specs=[VMEM] * 4,
        scratch_shapes=scratch,
        compiler_params=params,
        name="four_steps",
    )(info, strength, packed, *faces)

    if blocks == 2:
        own = swapped(advanced, sizes, lambda t, s: (1 - t, s))
    else:
        own = swapped(advanced, sizes, lambda t, s: (t + 1, s) if t + 1 < blocks else None)
    one, two, swap, below, above = halos(edge_one, edge_two, advanced, sizes, rows, place)
    flags = [block, place, swap, below, above]
    info = jnp.stack([jnp.asarray(flag).astype(jnp.int32) for flag in flags])
    result = pl.pallas_call(
        functools.partial(second_kernel, rows, width, layers),
        out_shape=struct(count, 2, layers, rows, lanes),
        in_specs=[SMEM] * 2 + [VMEM] * 12,
        out_specs=VMEM,
        scratch_shapes=scratch,
        compiler_params=params,
        name="three_steps",
    )(info, strength, packed, own, one, two, advanced, third, *faces)
    result = lax.all_to_all(result, "space", 0, 0, tiled=True)
    result = result.transpose(1, 2, 0, 3, 4).reshape(2, 1, layers, depth, lanes)
    return result[0], result[1]


def solution(mesh):
    sizes = tuple(mesh.shape[axis] for axis in AXES)
    in_specs = (
        P(("copy", "tm"), "space", None, None),
        P(("copy", "tm"), "space", None, None),
        P("space", None, None),
        P(None, "space", None, None),
        P("space", None, None),
        P("tm", None),
    )
    out_specs = (P(("copy", "tm"), "space", None, None), P(("copy", "tm"), "space", None, None))
    return jax.shard_map(
        functools.partial(shards, sizes), mesh=mesh, in_specs=in_specs, out_specs=out_specs, check_vma=False
    )
```

```python
import functools

import jax
import jax.numpy as jnp
from jax import lax
from jax.experimental import pallas as pl
from jax.experimental.pallas import tpu as pltpu
from jax.sharding import PartitionSpec as P

FINE = 4
LOW = 2 * FINE
lower_bound = 0.5
AXES = ("copy", "tm", "space")
VMEM = pl.BlockSpec(memory_space=pltpu.VMEM)
SMEM = pl.BlockSpec(memory_space=pltpu.SMEM)


def windows(values, place, rows, width):
    total, lanes = values.shape
    start = rows * place - LOW
    first, last = max(start, 0), min(start + width, total)
    parts = []
    if first > start:
        parts.append(jnp.zeros((first - start, lanes), values.dtype))
    parts.append(values[first:last])
    if last < start + width:
        parts.append(jnp.zeros((start + width - last, lanes), values.dtype))
    return jnp.concatenate(parts, axis=0) if len(parts) > 1 else parts[0]


def load_kernel(info, initial, source, diffusion, wind, buildings, strength, *rest):
    masked, winds, state, forcing, edge_one, edge_two, rates, fresh, early, late, solid, steps, sems = rest
    pairs = (
        (diffusion, fresh),
        (buildings, solid),
        (wind, winds),
        (initial.at[0], early),
        (source.at[0], late),
        (strength, steps),
    )
    copies = [pltpu.make_async_copy(*pair, sems.at[number]) for number, pair in enumerate(pairs)]
    for copy in copies:
        copy.start()
    for copy in copies[:3]:
        copy.wait()
    opened = (1 - solid[...]).astype(jnp.float32)
    masked[...] = fresh[...] * opened
    first, even = info[0] == 0, info[1] % 2 == 0
    last = masked.shape[0] - 1
    low = jnp.where(first, masked[0], winds[0, 0])
    high = jnp.where(first, masked[last], winds[0, last])
    edge_one[...] = jnp.where(even, high, low)
    edge_two[...] = jnp.where(even, low, high)
    for copy in copies[3:]:
        copy.wait()
    state[...] = early[...] * opened
    forcing[...] = late[...].astype(jnp.float32) * opened
    place = lax.broadcasted_iota(jnp.int32, rates.shape, 0)
    table = jnp.zeros(rates.shape, jnp.float32)
    for k in range(FINE):
        table = jnp.where(place == k, steps[0, k], table)
    rates[...] = table


def pack_shared(rows, width, info, masked, wind, same, across):
    first, spot, lead = info[0] == 0, info[1], info[4] == 0
    half = same.shape[0]
    swap = spot % 2 == 1
    for layer in range(masked.shape[0]):
        field = jnp.where(
            first,
            jnp.where(lead, masked[layer], wind[0, layer]),
            jnp.where(lead, wind[1, layer], wind[2, layer]),
        )
        for place in range(half):
            even = windows(field, 2 * place, rows, width)
            odd = windows(field, 2 * place + 1, rows, width)
            same[place ^ (spot // 2), layer] = jnp.where(swap, odd, even)
            across[place ^ (spot // 2), layer] = jnp.where(swap, even, odd)


def pack_own(rows, width, state, forcing, packed):
    layers = state.shape[0]
    for layer in range(layers):
        for spot in range(packed.shape[0]):
            packed[spot, pl.ds(layer * width, width)] = windows(state[layer], spot, rows, width)
            packed[spot, pl.ds((layers + layer) * width, width)] = windows(forcing[layer], spot, rows, width)


def bound_kernel(rows, width, info, rates, mine, other, masked, wind, state, forcing, out):
    first, even = info[0] == 0, info[1] % 2 == 0
    here, there = (mine[0], mine[1]), (other[0], other[1])

    def sides(one, two, keep):
        above, below = jnp.where(even, one, two), jnp.where(even, two, one)
        if keep:
            below, above = jnp.where(info[2] == 1, below, 0.0), jnp.where(info[3] == 1, above, 0.0)
        return below, above

    masked_sides = sides(jnp.where(first, here[0], there[0]), jnp.where(first, here[1], there[1]), True)
    wind_sides = sides(jnp.where(first, there[0], here[0]), jnp.where(first, there[1], here[1]), False)
    layers, depth, lanes = masked.shape
    chunk = 32 if depth % 32 == 0 else depth
    row = lax.broadcasted_iota(jnp.int32, (chunk, lanes), 0)
    inner_lane = lax.broadcasted_iota(jnp.int32, (chunk, lanes), 1) < lanes - 1

    def face(here, ahead, wind_here, wind_ahead):
        both = jnp.where((here > 0.0) & (ahead > 0.0), 1.0, 0.0)
        return jnp.sqrt(here * ahead), jnp.abs(0.5 * (wind_here + wind_ahead) * both)

    peaks = [jnp.zeros((chunk, lanes), jnp.float32)] * FINE
    edge = [[jnp.zeros((1, lanes), jnp.float32)] * 2 for _ in range(layers)]
    for start in range(0, depth, chunk):
        part = pl.ds(start, chunk)
        fields = [masked_sides[0][start : start + chunk]]
        fields += [masked[layer, part] for layer in range(layers)]
        fields += [masked_sides[1][start : start + chunk]]
        winds = [wind_sides[0][start : start + chunk]]
        winds += [wind[0, layer, part] for layer in range(layers)]
        winds += [wind_sides[1][start : start + chunk]]
        below = face(fields[0], fields[1], winds[0], winds[1])
        for layer in range(layers):
            field = fields[layer + 1]
            above = face(field, fields[layer + 2], winds[layer + 1], winds[layer + 2])
            sums = [above[0] + below[0], above[1] + below[1]]
            below = above
            flow = wind[1, layer, part]
            if start + chunk < depth:
                following = pl.ds(start + 1, chunk)
                pair = face(field, masked[layer, following], flow, wind[1, layer, following])
            else:
                pair = face(field, roll_back(field, 0), flow, roll_back(flow, 0))
                pair = [jnp.where(row < chunk - 1, value, 0.0) for value in pair]
            for number in range(2):
                value = pair[number]
                lower = jnp.where(row == 0, edge[layer][number], pltpu.roll(value, 1, 0))
                edge[layer][number] = value[chunk - 1 : chunk]
                sums[number] = sums[number] + value + lower
            flow = wind[2, layer, part]
            pair = face(field, roll_back(field, 1), flow, roll_back(flow, 1))
            for number in range(2):
                value = jnp.where(inner_lane, pair[number], 0.0)
                sums[number] = sums[number] + value + pltpu.roll(value, 1, 1)
            still = 1.0 + 2.0 * sums[0]
            for k in range(FINE):
                peaks[k] = jnp.maximum(peaks[k], still + rates[pl.ds(k, 1)] * sums[1])
    bounds = jnp.zeros((8, lanes), jnp.float32)
    place = lax.broadcasted_iota(jnp.int32, (8, lanes), 0)
    for k in range(FINE):
        bounds = jnp.where(place == k, jnp.max(peaks[k]), bounds)
    pack_own(rows, width, state, forcing, out)
    start = out.shape[1] - 8
    for spot in range(out.shape[0]):
        out[spot, pl.ds(start, 8)] = bounds


def roll_back(values, axis):
    return pltpu.roll(values, values.shape[axis] - 1, axis)


def face_kernel(info, mine, beside, other, other_beside, *faces):
    count, layers, width, lanes = mine.shape
    total = count * layers
    first, own, lead = info[0] == 0, info[1], info[4] == 0
    row = lax.broadcasted_iota(jnp.int32, (width, lanes), 0)
    lane = lax.broadcasted_iota(jnp.int32, (width, lanes), 1)
    inner_row = row < width - 1
    inner_lane = lane < lanes - 1
    zero = jnp.zeros((width, lanes), jnp.float32)

    def fields(place):
        spot, layer = (place // layers) ^ own, place % layers

        def ordered(one, two):
            one, two = one[spot, layer], two[spot, layer]
            return jnp.where(lead, one, two), jnp.where(lead, two, one)

        here, there = ordered(mine, beside), ordered(other, other_beside)
        masked = jnp.where(first, here[0], there[0])
        wind_x = jnp.where(first, here[1], there[1])
        wind_y = jnp.where(first, there[0], here[0])
        wind_z = jnp.where(first, there[1], here[1])
        return masked, wind_x, wind_y, wind_z

    def body(place, carry):
        masked, wind_x, wind_y, wind_z = carry
        following = fields(jnp.minimum(place + 1, total - 1))
        next_masked = jnp.where(place < total - 1, following[0], zero)
        opened = jnp.where(masked > 0.0, 1.0, 0.0)

        def face(masked_ahead, wind_here, wind_ahead, keep):
            conduct = jnp.sqrt(masked * masked_ahead)
            speed = 0.5 * (wind_here + wind_ahead) * opened * jnp.where(masked_ahead > 0.0, 1.0, 0.0)
            if keep is not None:
                conduct, speed = jnp.where(keep, conduct, 0.0), jnp.where(keep, speed, 0.0)
            return conduct, speed

        along_x = face(next_masked, wind_x, following[1], None)
        along_y = face(roll_back(masked, 0), wind_y, roll_back(wind_y, 0), inner_row)
        along_z = face(roll_back(masked, 1), wind_z, roll_back(wind_z, 1), inner_lane)
        for number, value in enumerate(along_x + along_y + along_z):
            faces[number][place] = value
        return next_masked, *following[1:]

    lax.fori_loop(0, total, body, fields(0), unroll=8)


def coefficients(bound):
    theta = (bound + lower_bound) * 0.5
    delta = (bound - lower_bound) * 0.5
    sigma = theta / delta
    rho_one = 1.0 / sigma
    rho_two = 1.0 / (2.0 * sigma - rho_one)
    beta = 2.0 * rho_two / (delta * theta)
    alpha = (1.0 + rho_one * rho_two) / theta + 2.0 * rho_two / delta
    return alpha - beta, beta


def one_step(total, width, layers, state, residual, ahead, faces, packed, rate, near, far):
    lanes = state.shape[-1]
    zero = jnp.zeros((width, lanes), jnp.float32)

    def difference(place, values, values_ahead, low_flow, pairs):
        flow_x = pairs[0] * values + pairs[1] * values_ahead
        flow_y = pairs[2] * values + pairs[3] * roll_back(values, 0)
        flow_z = pairs[4] * values + pairs[5] * roll_back(values, 1)
        change = (flow_x - low_flow) + (flow_y - pltpu.roll(flow_y, 1, 0)) + (flow_z - pltpu.roll(flow_z, 1, 1))
        return change, flow_x

    def first_sweep(place, carry):
        values, low_flow = carry
        values_ahead = state[place + 1]
        pairs = []
        for dim in range(3):
            conduct, speed = faces[2 * dim][place], faces[2 * dim + 1][place]
            pairs.append(conduct + rate * jnp.maximum(speed, 0.0))
            pairs.append(rate * jnp.minimum(speed, 0.0) - conduct)
        for number in range(6):
            ahead[number, place] = pairs[number]
        change, low_flow = difference(place, values, values_ahead, low_flow, pairs)
        spot, layer = place // layers, place % layers
        offset = pl.multiple_of((layers + layer) * width, 8)
        residual[place] = packed[spot, pl.ds(offset, width)] - change
        return values_ahead, low_flow

    def second_sweep(place, carry):
        values, low_flow = carry
        values_ahead = residual[place + 1]
        pairs = [ahead[number, place] for number in range(6)]
        change, low_flow = difference(place, values, values_ahead, low_flow, pairs)
        state[place] = state[place] + (near * values - far * change)
        return values_ahead, low_flow

    lax.fori_loop(0, total, first_sweep, (state[0], zero), unroll=8)
    lax.fori_loop(0, total, second_sweep, (residual[0], zero), unroll=8)


def bounds_of(packed):
    part = pl.ds(packed.shape[1] - 8, 8)
    bounds = packed[0, part]
    for entry in range(1, packed.shape[0]):
        bounds = jnp.maximum(bounds, packed[entry, part])
    return bounds


def first_kernel(rows, width, layers, info, rates, packed, *refs):
    faces, (advanced, third, edge_one, edge_two), (state, residual, ahead) = refs[:6], refs[6:10], refs[10:]
    total = state.shape[0] - 1
    zero = jnp.zeros(state.shape[1:], jnp.float32)
    state[total] = zero
    residual[total] = zero
    for place in range(total):
        state[place] = packed[place // layers, pl.ds(place % layers * width, width)]
    bounds = bounds_of(packed)
    for k in range(FINE):
        near, far = coefficients(bounds[k : k + 1])
        one_step(total, width, layers, state, residual, ahead, faces, packed, rates[pl.ds(k, 1)], near, far)
        if k == FINE - 2:
            third[...] = state[:total, LOW : LOW + rows]
    advanced[...] = state[:total, LOW : LOW + rows]
    edge = min(rows, LOW)
    low, high = state[:total, LOW : LOW + edge], state[:total, LOW + rows - edge : LOW + rows]
    even = info[1] % 2 == 0
    edge_one[...] = jnp.where(even, high, low)
    edge_two[...] = jnp.where(even, low, high)


def second_kernel(rows, width, layers, info, rates, packed, passed, halo_one, halo_two, advanced, third, *refs):
    faces, out, (state, residual, ahead) = refs[:6], refs[6], refs[7:]
    total = state.shape[0] - 1
    zero = jnp.zeros(state.shape[1:], jnp.float32)
    state[total] = zero
    residual[total] = zero
    swap = info[2] == 1
    below, above = halo_one[...], halo_two[...]
    low = jnp.where(swap, above, below)
    high = jnp.where(swap, below, above)
    state[:total, :LOW] = jnp.where(info[3] == 1, low, 0.0)
    state[:total, LOW : LOW + rows] = passed[...]
    state[:total, LOW + rows : 2 * LOW + rows] = jnp.where(info[4] == 1, high, 0.0)
    if width > 2 * LOW + rows:
        state[:total, 2 * LOW + rows :] = jnp.zeros((total, width - 2 * LOW - rows, state.shape[-1]), jnp.float32)
    bounds = bounds_of(packed)
    for k in range(FINE - 1):
        near, far = coefficients(bounds[k : k + 1])
        one_step(total, width, layers, state, residual, ahead, faces, packed, rates[pl.ds(k, 1)], near, far)
    first = info[0] == 0
    final = jnp.where(first, third[...], state[:total, LOW : LOW + rows])
    shape = out.shape[0:1] + out.shape[2:]
    out[:, 0] = advanced[...].reshape(shape)
    out[:, 1] = final.reshape(shape)


def swapped(array, sizes, partner, flip=0):
    copies, blocks, count = sizes
    pairs = []
    for c in range(copies):
        for t in range(blocks):
            for s in range(count):
                target = partner(t, s)
                if target is not None:
                    pairs.append(((c * blocks + t) * count + s, ((c ^ flip) * blocks + target[0]) * count + target[1]))
    return lax.ppermute(array, AXES, pairs)


def outer_partner(count):
    return lambda t, s: (t, ((s + 1) ^ 1) - 1) if 0 < s < count - 1 else (t ^ 1, s)


def halos(edge_one, edge_two, advanced, sizes, rows, place):
    copies, blocks, count = sizes
    even = place % 2 == 0
    below, above = place > 0, place < count - 1
    if rows >= LOW and blocks == 2 and count % 2 == 0:
        one = swapped(edge_one, sizes, lambda t, s: (1 - t, s ^ 1))
        two = swapped(edge_two, sizes, lambda t, s: (1 - t, ((s + 1) ^ 1) - 1 if 0 < s < count - 1 else s))
        return one, two, even, below, above

    def shifted(values, by):
        return swapped(
            values, sizes, lambda t, s: (t + 1, s + by) if t + 1 < blocks and 0 <= s + by < count else None
        )

    reach = -(-LOW // rows)
    low = jnp.concatenate([shifted(advanced, by) for by in range(reach, 0, -1)], axis=1)[:, -LOW:]
    high = jnp.concatenate([shifted(advanced, -by) for by in range(1, reach + 1)], axis=1)[:, :LOW]
    return low, high, False, True, True


def shards(sizes, initial, source, diffusion, wind_field, buildings, strength):
    copies, blocks, count = sizes
    layers, depth, lanes = diffusion.shape
    total, rows = layers * count, depth // count
    width = -(-(rows + 2 * LOW) // 8) * 8
    block, place = lax.axis_index("tm"), lax.axis_index("space")
    params = pltpu.CompilerParams(vmem_limit_bytes=48 * 1024 * 1024)

    def struct(*shape):
        return jax.ShapeDtypeStruct(shape, jnp.float32)

    def call(kernel, outs, in_specs, name, *operands, **options):
        return pl.pallas_call(
            kernel,
            out_shape=outs,
            in_specs=in_specs,
            out_specs=[VMEM] * len(outs),
            name=name,
            **{"compiler_params": params, **options},
        )(*operands)

    half = block % 2
    lead = lax.axis_index("copy") % 2
    flags = [half, place, place > 0, place < count - 1, lead]
    info = jnp.stack([jnp.asarray(flag).astype(jnp.int32) for flag in flags])
    slab = struct(layers, depth, lanes)
    outer = struct(depth, lanes)
    hold = pltpu.VMEM((layers, depth, lanes), jnp.float32)
    anywhere = pl.BlockSpec(memory_space=pltpu.HBM)
    arrays = (initial, source, diffusion, wind_field, buildings, strength)
    masked, winds, state, forcing, edge_one, edge_two, rates = call(
        load_kernel,
        [slab, struct(3, layers, depth, lanes), slab, slab, outer, outer, struct(8, lanes)],
        [SMEM] + [anywhere] * 6,
        "load",
        info,
        *(pltpu.with_memory_space_constraint(array, pltpu.HBM) for array in arrays),
        scratch_shapes=[
            hold,
            hold,
            pltpu.VMEM((layers, depth, lanes), source.dtype),
            pltpu.VMEM((layers, depth, lanes), jnp.int32),
            pltpu.SMEM(strength.shape, jnp.float32),
            pltpu.SemaphoreType.DMA((6,)),
        ],
    )
    edge_one = swapped(edge_one, sizes, lambda t, s: (t, s ^ 1))
    edge_two = swapped(edge_two, sizes, outer_partner(count))
    same, across = call(
        functools.partial(pack_shared, rows, width),
        [struct(count // 2, layers, width, lanes)] * 2,
        [SMEM] + [VMEM] * 2,
        "pack_shared",
        info,
        masked,
        winds,
    )
    across = swapped(across, sizes, lambda t, s: (t, s ^ 1))
    edges = jnp.stack([edge_one, edge_two])
    other_edges = swapped(edges, sizes, lambda t, s: (t ^ 1, s))
    (packed,) = call(
        functools.partial(bound_kernel, rows, width),
        [struct(count, 2 * layers * width + 8, lanes)],
        [SMEM] + [VMEM] * 7,
        "bounds",
        info,
        rates,
        edges,
        other_edges,
        masked,
        winds,
        state,
        forcing,
    )
    pieces = jnp.stack([same, across], axis=1)
    parts = [pieces[0]]
    for step in range(1, count // 2):
        parts.append(swapped(pieces[step], sizes, lambda t, s: (t, s ^ (2 * step))))
    *parts, _ = lax.optimization_barrier((*parts, packed))
    packed = lax.all_to_all(packed, "space", 0, 0, tiled=True)
    mine = jnp.concatenate(parts)
    beside = swapped(mine, sizes, lambda t, s: (t, s), 1)
    other = swapped(mine, sizes, lambda t, s: (t ^ 1, s))
    other_beside = swapped(beside, sizes, lambda t, s: (t ^ 1, s))
    faces = call(
        face_kernel,
        [struct(total, width, lanes)] * 6,
        [SMEM] + [VMEM] * 4,
        "faces",
        info,
        mine,
        beside,
        other,
        other_beside,
    )

    edge = min(rows, LOW)
    scratch = [
        pltpu.VMEM((total + 1, width, lanes), jnp.float32),
        pltpu.VMEM((total + 1, width, lanes), jnp.float32),
        pltpu.VMEM((6, total, width, lanes), jnp.float32),
    ]
    advanced, third, edge_one, edge_two = pl.pallas_call(
        functools.partial(first_kernel, rows, width, layers),
        out_shape=[struct(total, rows, lanes)] * 2 + [struct(total, edge, lanes)] * 2,
        in_specs=[SMEM] + [VMEM] * 8,
        out_specs=[VMEM] * 4,
        scratch_shapes=scratch,
        compiler_params=params,
        name="four_steps",
    )(info, rates, packed, *faces)

    if blocks == 2:
        own = swapped(advanced, sizes, lambda t, s: (1 - t, s))
    else:
        own = swapped(advanced, sizes, lambda t, s: (t + 1, s) if t + 1 < blocks else None)
    one, two, swap, below, above = halos(edge_one, edge_two, advanced, sizes, rows, place)
    flags = [block, place, swap, below, above]
    info = jnp.stack([jnp.asarray(flag).astype(jnp.int32) for flag in flags])
    result = pl.pallas_call(
        functools.partial(second_kernel, rows, width, layers),
        out_shape=struct(count, 2, layers, rows, lanes),
        in_specs=[SMEM] + [VMEM] * 13,
        out_specs=VMEM,
        scratch_shapes=scratch,
        compiler_params=params,
        name="three_steps",
    )(info, rates, packed, own, one, two, advanced, third, *faces)
    result = lax.all_to_all(result, "space", 0, 0, tiled=True)
    result = result.transpose(1, 2, 0, 3, 4).reshape(2, 1, layers, depth, lanes)
    return result[0], result[1]


def solution(mesh):
    sizes = tuple(mesh.shape[axis] for axis in AXES)
    in_specs = (
        P(("copy", "tm"), "space", None, None),
        P(("copy", "tm"), "space", None, None),
        P("space", None, None),
        P(None, "space", None, None),
        P("space", None, None),
        P("tm", None),
    )
    out_specs = (P(("copy", "tm"), "space", None, None), P(("copy", "tm"), "space", None, None))
    return jax.shard_map(
        functools.partial(shards, sizes), mesh=mesh, in_specs=in_specs, out_specs=out_specs, check_vma=False
    )
```

```python
import functools

import jax
import jax.numpy as jnp
from jax import lax
from jax.experimental import pallas as pl
from jax.experimental.pallas import tpu as pltpu
from jax.sharding import PartitionSpec as P

FINE = 4
LOW = 2 * FINE
lower_bound = 0.5
AXES = ("copy", "tm", "space")
VMEM = pl.BlockSpec(memory_space=pltpu.VMEM)
SMEM = pl.BlockSpec(memory_space=pltpu.SMEM)


def slab_of(place, count):
    return place ^ (place // 2 % 2) if count == 8 else place


def windows(values, place, rows, width):
    total, lanes = values.shape
    start = rows * place - LOW
    first, last = max(start, 0), min(start + width, total)
    parts = []
    if first > start:
        parts.append(jnp.zeros((first - start, lanes), values.dtype))
    parts.append(values[first:last])
    if last < start + width:
        parts.append(jnp.zeros((start + width - last, lanes), values.dtype))
    return jnp.concatenate(parts, axis=0) if len(parts) > 1 else parts[0]


def load_kernel(info, initial, source, diffusion, wind, buildings, strength, *rest):
    masked, winds, state, forcing, edge_one, edge_two, rates, fresh, early, late, solid, steps, sems = rest
    pairs = (
        (diffusion, fresh),
        (buildings, solid),
        (wind, winds),
        (initial.at[0], early),
        (source.at[0], late),
        (strength, steps),
    )
    copies = [pltpu.make_async_copy(*pair, sems.at[number]) for number, pair in enumerate(pairs)]
    for copy in copies:
        copy.start()
    for copy in copies[:3]:
        copy.wait()
    opened = (1 - solid[...]).astype(jnp.float32)
    masked[...] = fresh[...] * opened
    first, even = info[0] == 0, info[1] % 2 == 0
    last = masked.shape[0] - 1
    low = jnp.where(first, masked[0], winds[0, 0])
    high = jnp.where(first, masked[last], winds[0, last])
    edge_one[...] = jnp.where(even, high, low)
    edge_two[...] = jnp.where(even, low, high)
    for copy in copies[3:]:
        copy.wait()
    state[...] = early[...] * opened
    forcing[...] = late[...].astype(jnp.float32) * opened
    place = lax.broadcasted_iota(jnp.int32, rates.shape, 0)
    table = jnp.zeros(rates.shape, jnp.float32)
    for k in range(FINE):
        table = jnp.where(place == k, steps[0, k], table)
    rates[...] = table


def pack_shared(rows, width, info, masked, wind, same, across):
    first, spot, lead = info[0] == 0, info[1], info[4] == 0
    half = same.shape[0]
    swap = spot % 2 == 1
    for layer in range(masked.shape[0]):
        field = jnp.where(
            first,
            jnp.where(lead, masked[layer], wind[0, layer]),
            jnp.where(lead, wind[1, layer], wind[2, layer]),
        )
        for place in range(half):
            even = windows(field, slab_of(2 * place, 2 * half), rows, width)
            odd = windows(field, slab_of(2 * place + 1, 2 * half), rows, width)
            same[place ^ (spot // 2), layer] = jnp.where(swap, odd, even)
            across[place ^ (spot // 2), layer] = jnp.where(swap, even, odd)


def pack_own(rows, width, state, forcing, packed):
    layers = state.shape[0]
    for layer in range(layers):
        for spot in range(packed.shape[0]):
            packed[spot, pl.ds(layer * width, width)] = windows(state[layer], slab_of(spot, packed.shape[0]), rows, width)
            packed[spot, pl.ds((layers + layer) * width, width)] = windows(forcing[layer], slab_of(spot, packed.shape[0]), rows, width)


def bound_kernel(rows, width, info, rates, mine, other, masked, wind, state, forcing, out):
    first, even = info[0] == 0, info[1] % 2 == 0
    here, there = (mine[0], mine[1]), (other[0], other[1])

    def sides(one, two, keep):
        above, below = jnp.where(even, one, two), jnp.where(even, two, one)
        if keep:
            below, above = jnp.where(info[2] == 1, below, 0.0), jnp.where(info[3] == 1, above, 0.0)
        return below, above

    masked_sides = sides(jnp.where(first, here[0], there[0]), jnp.where(first, here[1], there[1]), True)
    wind_sides = sides(jnp.where(first, there[0], here[0]), jnp.where(first, there[1], here[1]), False)
    layers, depth, lanes = masked.shape
    chunk = 32 if depth % 32 == 0 else depth
    row = lax.broadcasted_iota(jnp.int32, (chunk, lanes), 0)
    inner_lane = lax.broadcasted_iota(jnp.int32, (chunk, lanes), 1) < lanes - 1

    def face(here, ahead, wind_here, wind_ahead):
        both = jnp.where((here > 0.0) & (ahead > 0.0), 1.0, 0.0)
        return jnp.sqrt(here * ahead), jnp.abs(0.5 * (wind_here + wind_ahead) * both)

    peaks = [jnp.zeros((chunk, lanes), jnp.float32)] * FINE
    edge = [[jnp.zeros((1, lanes), jnp.float32)] * 2 for _ in range(layers)]
    for start in range(0, depth, chunk):
        part = pl.ds(start, chunk)
        fields = [masked_sides[0][start : start + chunk]]
        fields += [masked[layer, part] for layer in range(layers)]
        fields += [masked_sides[1][start : start + chunk]]
        winds = [wind_sides[0][start : start + chunk]]
        winds += [wind[0, layer, part] for layer in range(layers)]
        winds += [wind_sides[1][start : start + chunk]]
        below = face(fields[0], fields[1], winds[0], winds[1])
        for layer in range(layers):
            field = fields[layer + 1]
            above = face(field, fields[layer + 2], winds[layer + 1], winds[layer + 2])
            sums = [above[0] + below[0], above[1] + below[1]]
            below = above
            flow = wind[1, layer, part]
            if start + chunk < depth:
                following = pl.ds(start + 1, chunk)
                pair = face(field, masked[layer, following], flow, wind[1, layer, following])
            else:
                pair = face(field, roll_back(field, 0), flow, roll_back(flow, 0))
                pair = [jnp.where(row < chunk - 1, value, 0.0) for value in pair]
            for number in range(2):
                value = pair[number]
                lower = jnp.where(row == 0, edge[layer][number], pltpu.roll(value, 1, 0))
                edge[layer][number] = value[chunk - 1 : chunk]
                sums[number] = sums[number] + value + lower
            flow = wind[2, layer, part]
            pair = face(field, roll_back(field, 1), flow, roll_back(flow, 1))
            for number in range(2):
                value = jnp.where(inner_lane, pair[number], 0.0)
                sums[number] = sums[number] + value + pltpu.roll(value, 1, 1)
            still = 1.0 + 2.0 * sums[0]
            for k in range(FINE):
                peaks[k] = jnp.maximum(peaks[k], still + rates[pl.ds(k, 1)] * sums[1])
    bounds = jnp.zeros((8, lanes), jnp.float32)
    place = lax.broadcasted_iota(jnp.int32, (8, lanes), 0)
    for k in range(FINE):
        bounds = jnp.where(place == k, jnp.max(peaks[k]), bounds)
    pack_own(rows, width, state, forcing, out)
    start = out.shape[1] - 8
    for spot in range(out.shape[0]):
        out[spot, pl.ds(start, 8)] = bounds


def roll_back(values, axis):
    return pltpu.roll(values, values.shape[axis] - 1, axis)


def face_kernel(info, mine, beside, other, other_beside, *faces):
    count, layers, width, lanes = mine.shape
    total = count * layers
    first, own, lead = info[0] == 0, info[1], info[4] == 0
    row = lax.broadcasted_iota(jnp.int32, (width, lanes), 0)
    lane = lax.broadcasted_iota(jnp.int32, (width, lanes), 1)
    inner_row = row < width - 1
    inner_lane = lane < lanes - 1
    zero = jnp.zeros((width, lanes), jnp.float32)

    def fields(place):
        spot, layer = (place // layers) ^ own, place % layers

        def ordered(one, two):
            one, two = one[spot, layer], two[spot, layer]
            return jnp.where(lead, one, two), jnp.where(lead, two, one)

        here, there = ordered(mine, beside), ordered(other, other_beside)
        masked = jnp.where(first, here[0], there[0])
        wind_x = jnp.where(first, here[1], there[1])
        wind_y = jnp.where(first, there[0], here[0])
        wind_z = jnp.where(first, there[1], here[1])
        return masked, wind_x, wind_y, wind_z

    def body(place, carry):
        masked, wind_x, wind_y, wind_z = carry
        following = fields(jnp.minimum(place + 1, total - 1))
        next_masked = jnp.where(place < total - 1, following[0], zero)
        opened = jnp.where(masked > 0.0, 1.0, 0.0)

        def face(masked_ahead, wind_here, wind_ahead, keep):
            conduct = jnp.sqrt(masked * masked_ahead)
            speed = 0.5 * (wind_here + wind_ahead) * opened * jnp.where(masked_ahead > 0.0, 1.0, 0.0)
            if keep is not None:
                conduct, speed = jnp.where(keep, conduct, 0.0), jnp.where(keep, speed, 0.0)
            return conduct, speed

        along_x = face(next_masked, wind_x, following[1], None)
        along_y = face(roll_back(masked, 0), wind_y, roll_back(wind_y, 0), inner_row)
        along_z = face(roll_back(masked, 1), wind_z, roll_back(wind_z, 1), inner_lane)
        for number, value in enumerate(along_x + along_y + along_z):
            faces[number][place] = value
        return next_masked, *following[1:]

    lax.fori_loop(0, total, body, fields(0), unroll=8)


def coefficients(bound):
    theta = (bound + lower_bound) * 0.5
    delta = (bound - lower_bound) * 0.5
    sigma = theta / delta
    rho_one = 1.0 / sigma
    rho_two = 1.0 / (2.0 * sigma - rho_one)
    beta = 2.0 * rho_two / (delta * theta)
    alpha = (1.0 + rho_one * rho_two) / theta + 2.0 * rho_two / delta
    return alpha - beta, beta


def one_step(total, width, layers, state, residual, ahead, faces, packed, rate, near, far):
    lanes = state.shape[-1]
    zero = jnp.zeros((width, lanes), jnp.float32)

    def difference(place, values, values_ahead, low_flow, pairs):
        flow_x = pairs[0] * values + pairs[1] * values_ahead
        flow_y = pairs[2] * values + pairs[3] * roll_back(values, 0)
        flow_z = pairs[4] * values + pairs[5] * roll_back(values, 1)
        change = (flow_x - low_flow) + (flow_y - pltpu.roll(flow_y, 1, 0)) + (flow_z - pltpu.roll(flow_z, 1, 1))
        return change, flow_x

    def first_sweep(place, carry):
        values, low_flow = carry
        values_ahead = state[place + 1]
        pairs = []
        for dim in range(3):
            conduct, speed = faces[2 * dim][place], faces[2 * dim + 1][place]
            speed = rate * speed
            pairs.append(conduct + jnp.maximum(speed, 0.0))
            pairs.append(jnp.minimum(speed, 0.0) - conduct)
        for number in range(6):
            ahead[number, place] = pairs[number]
        change, low_flow = difference(place, values, values_ahead, low_flow, pairs)
        spot, layer = place // layers, place % layers
        offset = pl.multiple_of((layers + layer) * width, 8)
        residual[place] = packed[spot, pl.ds(offset, width)] - change
        return values_ahead, low_flow

    def second_sweep(place, carry):
        values, low_flow = carry
        values_ahead = residual[place + 1]
        pairs = [ahead[number, place] for number in range(6)]
        change, low_flow = difference(place, values, values_ahead, low_flow, pairs)
        state[place] = state[place] + (near * values - far * change)
        return values_ahead, low_flow

    lax.fori_loop(0, total, first_sweep, (state[0], zero), unroll=8)
    lax.fori_loop(0, total, second_sweep, (residual[0], zero), unroll=16)


def bounds_of(packed):
    part = pl.ds(packed.shape[1] - 8, 8)
    bounds = packed[0, part]
    for entry in range(1, packed.shape[0]):
        bounds = jnp.maximum(bounds, packed[entry, part])
    return bounds


def first_kernel(rows, width, layers, info, rates, packed, *refs):
    faces, (advanced, third, edge_one, edge_two), (state, residual, ahead) = refs[:6], refs[6:10], refs[10:]
    total = state.shape[0] - 1
    zero = jnp.zeros(state.shape[1:], jnp.float32)
    state[total] = zero
    residual[total] = zero
    for place in range(total):
        state[place] = packed[place // layers, pl.ds(place % layers * width, width)]
    bounds = bounds_of(packed)
    for k in range(FINE):
        near, far = coefficients(bounds[k : k + 1])
        one_step(total, width, layers, state, residual, ahead, faces, packed, rates[pl.ds(k, 1)], near, far)
        if k == FINE - 2:
            third[...] = state[:total, LOW : LOW + rows]
    advanced[...] = state[:total, LOW : LOW + rows]
    edge = min(rows, LOW)
    low, high = state[:total, LOW : LOW + edge], state[:total, LOW + rows - edge : LOW + rows]
    even = info[5] % 2 == 0
    edge_one[...] = jnp.where(even, high, low)
    edge_two[...] = jnp.where(even, low, high)


def second_kernel(rows, width, layers, info, rates, packed, passed, halo_one, halo_two, advanced, third, *refs):
    faces, out, (state, residual, ahead) = refs[:6], refs[6], refs[7:]
    total = state.shape[0] - 1
    zero = jnp.zeros(state.shape[1:], jnp.float32)
    state[total] = zero
    residual[total] = zero
    swap = info[2] == 1
    below, above = halo_one[...], halo_two[...]
    low = jnp.where(swap, above, below)
    high = jnp.where(swap, below, above)
    state[:total, :LOW] = jnp.where(info[3] == 1, low, 0.0)
    state[:total, LOW : LOW + rows] = passed[...]
    state[:total, LOW + rows : 2 * LOW + rows] = jnp.where(info[4] == 1, high, 0.0)
    if width > 2 * LOW + rows:
        state[:total, 2 * LOW + rows :] = jnp.zeros((total, width - 2 * LOW - rows, state.shape[-1]), jnp.float32)
    bounds = bounds_of(packed)
    for k in range(FINE - 1):
        near, far = coefficients(bounds[k : k + 1])
        one_step(total, width, layers, state, residual, ahead, faces, packed, rates[pl.ds(k, 1)], near, far)
    first = info[0] == 0
    final = jnp.where(first, third[...], state[:total, LOW : LOW + rows])
    shape = out.shape[0:1] + out.shape[2:]
    out[:, 0] = advanced[...].reshape(shape)
    out[:, 1] = final.reshape(shape)


def unpack_kernel(result, *refs):
    outs, sems = refs[:2], refs[2]
    count, rows = result.shape[0], result.shape[3]
    copies = []
    for number, out in enumerate(outs):
        for spot in range(count):
            target = out.at[0, :, pl.ds(slab_of(spot, count) * rows, rows)]
            copies.append(pltpu.make_async_copy(result.at[spot, number], target, sems.at[number, spot]))
    for copy in copies:
        copy.start()
    for copy in copies:
        copy.wait()


def swapped(array, sizes, partner, flip=0):
    copies, blocks, count = sizes
    pairs = []
    for c in range(copies):
        for t in range(blocks):
            for s in range(count):
                target = partner(t, s)
                if target is not None:
                    pairs.append(((c * blocks + t) * count + s, ((c ^ flip) * blocks + target[0]) * count + target[1]))
    return lax.ppermute(array, AXES, pairs)


def outer_partner(count):
    return lambda t, s: (t, ((s + 1) ^ 1) - 1) if 0 < s < count - 1 else (t ^ 1, s)


def halos(edge_one, edge_two, advanced, sizes, rows, slab):
    copies, blocks, count = sizes
    even = slab % 2 == 0
    below, above = slab > 0, slab < count - 1
    if rows >= LOW and blocks == 2 and count % 2 == 0:
        def partner(t, s):
            own = slab_of(s, count)
            return 1 - t, slab_of(((own + 1) ^ 1) - 1, count) if 0 < own < count - 1 else s

        one = swapped(edge_one, sizes, lambda t, s: (1 - t, s ^ 1))
        two = swapped(edge_two, sizes, partner)
        return one, two, even, below, above

    def shifted(values, by):
        return swapped(
            values, sizes, lambda t, s: (t + 1, s + by) if t + 1 < blocks and 0 <= s + by < count else None
        )

    reach = -(-LOW // rows)
    low = jnp.concatenate([shifted(advanced, by) for by in range(reach, 0, -1)], axis=1)[:, -LOW:]
    high = jnp.concatenate([shifted(advanced, -by) for by in range(1, reach + 1)], axis=1)[:, :LOW]
    return low, high, False, True, True


def shards(sizes, initial, source, diffusion, wind_field, buildings, strength):
    copies, blocks, count = sizes
    layers, depth, lanes = diffusion.shape
    total, rows = layers * count, depth // count
    width = -(-(rows + 2 * LOW) // 8) * 8
    block, place = lax.axis_index("tm"), lax.axis_index("space")
    params = pltpu.CompilerParams(vmem_limit_bytes=48 * 1024 * 1024)

    def struct(*shape):
        return jax.ShapeDtypeStruct(shape, jnp.float32)

    def call(kernel, outs, in_specs, name, *operands, **options):
        return pl.pallas_call(
            kernel,
            out_shape=outs,
            in_specs=in_specs,
            out_specs=[VMEM] * len(outs),
            name=name,
            **{"compiler_params": params, **options},
        )(*operands)

    half = block % 2
    lead = lax.axis_index("copy") % 2
    slab = slab_of(place, count)
    flags = [half, place, place > 0, place < count - 1, lead, slab]
    info = jnp.stack([jnp.asarray(flag).astype(jnp.int32) for flag in flags])
    field = struct(layers, depth, lanes)
    outer = struct(depth, lanes)
    hold = pltpu.VMEM((layers, depth, lanes), jnp.float32)
    anywhere = pl.BlockSpec(memory_space=pltpu.HBM)
    arrays = (initial, source, diffusion, wind_field, buildings, strength)
    masked, winds, state, forcing, edge_one, edge_two, rates = call(
        load_kernel,
        [field, struct(3, layers, depth, lanes), field, field, outer, outer, struct(8, lanes)],
        [SMEM] + [anywhere] * 6,
        "load",
        info,
        *(pltpu.with_memory_space_constraint(array, pltpu.HBM) for array in arrays),
        scratch_shapes=[
            hold,
            hold,
            pltpu.VMEM((layers, depth, lanes), source.dtype),
            pltpu.VMEM((layers, depth, lanes), jnp.int32),
            pltpu.SMEM(strength.shape, jnp.float32),
            pltpu.SemaphoreType.DMA((6,)),
        ],
    )
    same, across = call(
        functools.partial(pack_shared, rows, width),
        [struct(count // 2, layers, width, lanes)] * 2,
        [SMEM] + [VMEM] * 2,
        "pack_shared",
        info,
        masked,
        winds,
    )
    across = swapped(across, sizes, lambda t, s: (t, s ^ 1))
    edge_one = swapped(edge_one, sizes, lambda t, s: (t, s ^ 1))
    edge_two = swapped(edge_two, sizes, outer_partner(count))
    edges = jnp.stack([edge_one, edge_two])
    other_edges = swapped(edges, sizes, lambda t, s: (t ^ 1, s))
    (packed,) = call(
        functools.partial(bound_kernel, rows, width),
        [struct(count, 2 * layers * width + 8, lanes)],
        [SMEM] + [VMEM] * 7,
        "bounds",
        info,
        rates,
        edges,
        other_edges,
        masked,
        winds,
        state,
        forcing,
    )
    pieces = jnp.stack([same, across], axis=1)
    parts = [pieces[0]]
    for step in range(1, count // 2):
        parts.append(swapped(pieces[step], sizes, lambda t, s: (t, s ^ (2 * step))))
    *parts, _ = lax.optimization_barrier((*parts, packed))
    packed = lax.all_to_all(packed, "space", 0, 0, tiled=True)
    mine = jnp.concatenate(parts)
    beside = swapped(mine, sizes, lambda t, s: (t, s), 1)
    other = swapped(mine, sizes, lambda t, s: (t ^ 1, s))
    other_beside = swapped(beside, sizes, lambda t, s: (t ^ 1, s))
    faces = call(
        face_kernel,
        [struct(total, width, lanes)] * 6,
        [SMEM] + [VMEM] * 4,
        "faces",
        info,
        mine,
        beside,
        other,
        other_beside,
    )

    edge = min(rows, LOW)
    scratch = [
        pltpu.VMEM((total + 1, width, lanes), jnp.float32),
        pltpu.VMEM((total + 1, width, lanes), jnp.float32),
        pltpu.VMEM((6, total, width, lanes), jnp.float32),
    ]
    advanced, third, edge_one, edge_two = pl.pallas_call(
        functools.partial(first_kernel, rows, width, layers),
        out_shape=[struct(total, rows, lanes)] * 2 + [struct(total, edge, lanes)] * 2,
        in_specs=[SMEM] + [VMEM] * 8,
        out_specs=[VMEM] * 4,
        scratch_shapes=scratch,
        compiler_params=params,
        name="four_steps",
    )(info, rates, packed, *faces)

    if blocks == 2:
        own = swapped(advanced, sizes, lambda t, s: (1 - t, s))
    else:
        own = swapped(advanced, sizes, lambda t, s: (t + 1, s) if t + 1 < blocks else None)
    one, two, swap, below, above = halos(edge_one, edge_two, advanced, sizes, rows, slab)
    flags = [block, place, swap, below, above]
    info = jnp.stack([jnp.asarray(flag).astype(jnp.int32) for flag in flags])
    result = pl.pallas_call(
        functools.partial(second_kernel, rows, width, layers),
        out_shape=struct(count, 2, layers, rows, lanes),
        in_specs=[SMEM] + [VMEM] * 13,
        out_specs=VMEM,
        scratch_shapes=scratch,
        compiler_params=params,
        name="three_steps",
    )(info, rates, packed, own, one, two, advanced, third, *faces)
    result = lax.all_to_all(result, "space", 0, 0, tiled=True)
    if rows % 8:
        result = result.transpose(1, 2, 0, 3, 4).reshape(2, 1, layers, depth, lanes)
        return result[0], result[1]
    return tuple(
        pl.pallas_call(
            unpack_kernel,
            out_shape=[struct(1, layers, depth, lanes)] * 2,
            in_specs=[VMEM],
            out_specs=[pl.BlockSpec(memory_space=pl.ANY)] * 2,
            scratch_shapes=[pltpu.SemaphoreType.DMA((2, count))],
            compiler_params=params,
            name="unpack",
        )(result)
    )


def solution(mesh):
    sizes = tuple(mesh.shape[axis] for axis in AXES)
    in_specs = (
        P(("copy", "tm"), "space", None, None),
        P(("copy", "tm"), "space", None, None),
        P("space", None, None),
        P(None, "space", None, None),
        P("space", None, None),
        P("tm", None),
    )
    out_specs = (P(("copy", "tm"), "space", None, None), P(("copy", "tm"), "space", None, None))
    return jax.shard_map(
        functools.partial(shards, sizes), mesh=mesh, in_specs=in_specs, out_specs=out_specs, check_vma=False
    )
```

```python
import functools

import jax
import jax.numpy as jnp
from jax import lax
from jax.experimental import pallas as pl
from jax.experimental.pallas import tpu as pltpu
from jax.sharding import PartitionSpec as P

FINE = 4
LOW = 2 * FINE
lower_bound = 0.5
AXES = ("copy", "tm", "space")
VMEM = pl.BlockSpec(memory_space=pltpu.VMEM)
SMEM = pl.BlockSpec(memory_space=pltpu.SMEM)


def slab_of(place, count):
    return place ^ (place // 2 % 2) if count == 8 else place


def windows(values, place, rows, width):
    total, lanes = values.shape
    start = rows * place - LOW
    first, last = max(start, 0), min(start + width, total)
    parts = []
    if first > start:
        parts.append(jnp.zeros((first - start, lanes), values.dtype))
    parts.append(values[first:last])
    if last < start + width:
        parts.append(jnp.zeros((start + width - last, lanes), values.dtype))
    return jnp.concatenate(parts, axis=0) if len(parts) > 1 else parts[0]


def load_kernel(info, initial, source, diffusion, wind, buildings, strength, *rest):
    masked, winds, state, forcing, edge_one, edge_two, rates, fresh, early, late, solid, steps, sems = rest
    pairs = (
        (diffusion, fresh),
        (buildings, solid),
        (wind, winds),
        (initial.at[0], early),
        (source.at[0], late),
        (strength, steps),
    )
    copies = [pltpu.make_async_copy(*pair, sems.at[number]) for number, pair in enumerate(pairs)]
    for copy in copies:
        copy.start()
    for copy in copies[:3]:
        copy.wait()
    opened = (1 - solid[...]).astype(jnp.float32)
    masked[...] = fresh[...] * opened
    first, even = info[0] == 0, info[1] % 2 == 0
    last = masked.shape[0] - 1
    low = jnp.where(first, masked[0], winds[0, 0])
    high = jnp.where(first, masked[last], winds[0, last])
    edge_one[...] = jnp.where(even, high, low)
    edge_two[...] = jnp.where(even, low, high)
    for copy in copies[3:]:
        copy.wait()
    state[...] = early[...] * opened
    forcing[...] = late[...].astype(jnp.float32) * opened
    place = lax.broadcasted_iota(jnp.int32, rates.shape, 0)
    table = jnp.zeros(rates.shape, jnp.float32)
    for k in range(FINE):
        table = jnp.where(place == k, steps[0, k], table)
    rates[...] = table


def pack_shared(rows, width, info, masked, wind, same, across):
    first, spot, lead = info[0] == 0, info[1], info[4] == 0
    half = same.shape[0]
    swap = spot % 2 == 1
    for layer in range(masked.shape[0]):
        field = jnp.where(
            first,
            jnp.where(lead, masked[layer], wind[0, layer]),
            jnp.where(lead, wind[1, layer], wind[2, layer]),
        )
        for place in range(half):
            even = windows(field, slab_of(2 * place, 2 * half), rows, width)
            odd = windows(field, slab_of(2 * place + 1, 2 * half), rows, width)
            same[place ^ (spot // 2), layer] = jnp.where(swap, odd, even)
            across[place ^ (spot // 2), layer] = jnp.where(swap, even, odd)


def pack_own(rows, width, state, forcing, packed):
    layers = state.shape[0]
    for layer in range(layers):
        for spot in range(packed.shape[0]):
            packed[spot, pl.ds(layer * width, width)] = windows(state[layer], slab_of(spot, packed.shape[0]), rows, width)
            packed[spot, pl.ds((layers + layer) * width, width)] = windows(forcing[layer], slab_of(spot, packed.shape[0]), rows, width)


def bound_kernel(rows, width, info, rates, mine, other, masked, wind, state, forcing, out):
    first, even = info[0] == 0, info[1] % 2 == 0
    here, there = (mine[0], mine[1]), (other[0], other[1])

    def sides(one, two, keep):
        above, below = jnp.where(even, one, two), jnp.where(even, two, one)
        if keep:
            below, above = jnp.where(info[2] == 1, below, 0.0), jnp.where(info[3] == 1, above, 0.0)
        return below, above

    masked_sides = sides(jnp.where(first, here[0], there[0]), jnp.where(first, here[1], there[1]), True)
    wind_sides = sides(jnp.where(first, there[0], here[0]), jnp.where(first, there[1], here[1]), False)
    layers, depth, lanes = masked.shape
    chunk = 32 if depth % 32 == 0 else depth
    row = lax.broadcasted_iota(jnp.int32, (chunk, lanes), 0)
    inner_lane = lax.broadcasted_iota(jnp.int32, (chunk, lanes), 1) < lanes - 1

    def face(here, ahead, wind_here, wind_ahead):
        both = jnp.where((here > 0.0) & (ahead > 0.0), 1.0, 0.0)
        return jnp.sqrt(here * ahead), jnp.abs(0.5 * (wind_here + wind_ahead) * both)

    peaks = [jnp.zeros((chunk, lanes), jnp.float32)] * FINE
    edge = [[jnp.zeros((1, lanes), jnp.float32)] * 2 for _ in range(layers)]
    for start in range(0, depth, chunk):
        part = pl.ds(start, chunk)
        fields = [masked_sides[0][start : start + chunk]]
        fields += [masked[layer, part] for layer in range(layers)]
        fields += [masked_sides[1][start : start + chunk]]
        winds = [wind_sides[0][start : start + chunk]]
        winds += [wind[0, layer, part] for layer in range(layers)]
        winds += [wind_sides[1][start : start + chunk]]
        below = face(fields[0], fields[1], winds[0], winds[1])
        for layer in range(layers):
            field = fields[layer + 1]
            above = face(field, fields[layer + 2], winds[layer + 1], winds[layer + 2])
            sums = [above[0] + below[0], above[1] + below[1]]
            below = above
            flow = wind[1, layer, part]
            if start + chunk < depth:
                following = pl.ds(start + 1, chunk)
                pair = face(field, masked[layer, following], flow, wind[1, layer, following])
            else:
                pair = face(field, roll_back(field, 0), flow, roll_back(flow, 0))
                pair = [jnp.where(row < chunk - 1, value, 0.0) for value in pair]
            for number in range(2):
                value = pair[number]
                lower = jnp.where(row == 0, edge[layer][number], pltpu.roll(value, 1, 0))
                edge[layer][number] = value[chunk - 1 : chunk]
                sums[number] = sums[number] + value + lower
            flow = wind[2, layer, part]
            pair = face(field, roll_back(field, 1), flow, roll_back(flow, 1))
            for number in range(2):
                value = jnp.where(inner_lane, pair[number], 0.0)
                sums[number] = sums[number] + value + pltpu.roll(value, 1, 1)
            still = 1.0 + 2.0 * sums[0]
            for k in range(FINE):
                peaks[k] = jnp.maximum(peaks[k], still + rates[pl.ds(k, 1)] * sums[1])
    bounds = jnp.zeros((8, lanes), jnp.float32)
    place = lax.broadcasted_iota(jnp.int32, (8, lanes), 0)
    for k in range(FINE):
        bounds = jnp.where(place == k, jnp.max(peaks[k]), bounds)
    pack_own(rows, width, state, forcing, out)
    start = out.shape[1] - 8
    for spot in range(out.shape[0]):
        out[spot, pl.ds(start, 8)] = bounds


def roll_back(values, axis):
    return pltpu.roll(values, values.shape[axis] - 1, axis)


def face_kernel(info, mine, beside, other, other_beside, *faces):
    count, layers, width, lanes = mine.shape
    total = count * layers
    first, own, lead = info[0] == 0, info[1], info[4] == 0
    row = lax.broadcasted_iota(jnp.int32, (width, lanes), 0)
    lane = lax.broadcasted_iota(jnp.int32, (width, lanes), 1)
    inner_row = row < width - 1
    inner_lane = lane < lanes - 1
    zero = jnp.zeros((width, lanes), jnp.float32)

    def fields(place):
        spot, layer = (place // layers) ^ own, place % layers

        def ordered(one, two):
            one, two = one[spot, layer], two[spot, layer]
            return jnp.where(lead, one, two), jnp.where(lead, two, one)

        here, there = ordered(mine, beside), ordered(other, other_beside)
        masked = jnp.where(first, here[0], there[0])
        wind_x = jnp.where(first, here[1], there[1])
        wind_y = jnp.where(first, there[0], here[0])
        wind_z = jnp.where(first, there[1], here[1])
        return masked, wind_x, wind_y, wind_z

    def body(place, carry):
        masked, wind_x, wind_y, wind_z = carry
        following = fields(jnp.minimum(place + 1, total - 1))
        next_masked = jnp.where(place < total - 1, following[0], zero)
        opened = jnp.where(masked > 0.0, 1.0, 0.0)

        def face(masked_ahead, wind_here, wind_ahead, keep):
            conduct = jnp.sqrt(masked * masked_ahead)
            speed = 0.5 * (wind_here + wind_ahead) * opened * jnp.where(masked_ahead > 0.0, 1.0, 0.0)
            if keep is not None:
                conduct, speed = jnp.where(keep, conduct, 0.0), jnp.where(keep, speed, 0.0)
            return conduct, speed

        along_x = face(next_masked, wind_x, following[1], None)
        along_y = face(roll_back(masked, 0), wind_y, roll_back(wind_y, 0), inner_row)
        along_z = face(roll_back(masked, 1), wind_z, roll_back(wind_z, 1), inner_lane)
        for number, value in enumerate(along_x + along_y + along_z):
            faces[number][place] = value
        return next_masked, *following[1:]

    lax.fori_loop(0, total, body, fields(0), unroll=8)


def coefficients(bound):
    theta = (bound + lower_bound) * 0.5
    delta = (bound - lower_bound) * 0.5
    sigma = theta / delta
    rho_one = 1.0 / sigma
    rho_two = 1.0 / (2.0 * sigma - rho_one)
    beta = 2.0 * rho_two / (delta * theta)
    alpha = (1.0 + rho_one * rho_two) / theta + 2.0 * rho_two / delta
    return alpha - beta, beta


def one_step(total, width, layers, state, result, residual, ahead, faces, packed, rate, near, far, rows=0, store=None):
    lanes = state.shape[-1]
    zero = jnp.zeros((width, lanes), jnp.float32)

    def difference(place, values, values_ahead, low_flow, pairs):
        flow_x = pairs[0] * values + pairs[1] * values_ahead
        flow_y = pairs[2] * values + pairs[3] * roll_back(values, 0)
        flow_z = pairs[4] * values + pairs[5] * roll_back(values, 1)
        change = (flow_x - low_flow) + (flow_y - pltpu.roll(flow_y, 1, 0)) + (flow_z - pltpu.roll(flow_z, 1, 1))
        return change, flow_x

    def first_sweep(place, carry):
        values, low_flow = carry
        values_ahead = state[place + 1]
        pairs = []
        for dim in range(3):
            conduct, speed = faces[2 * dim][place], faces[2 * dim + 1][place]
            speed = rate * speed
            pairs.append(conduct + jnp.maximum(speed, 0.0))
            pairs.append(jnp.minimum(speed, 0.0) - conduct)
        for number in range(6):
            ahead[number, place] = pairs[number]
        change, low_flow = difference(place, values, values_ahead, low_flow, pairs)
        spot, layer = place // layers, place % layers
        offset = pl.multiple_of((layers + layer) * width, 8)
        residual[place] = packed[spot, pl.ds(offset, width)] - change
        return values_ahead, low_flow

    def second_sweep(place, carry):
        values, low_flow = carry
        values_ahead = residual[place + 1]
        pairs = [ahead[number, place] for number in range(6)]
        change, low_flow = difference(place, values, values_ahead, low_flow, pairs)
        result[place] = state[place] + (near * values - far * change)
        return values_ahead, low_flow

    lax.fori_loop(0, total, first_sweep, (state[0], zero), unroll=8)
    inner, below, above = pl.ds(LOW, rows), pl.ds(LOW - 1, rows), pl.ds(LOW + 1, rows)

    def inner_sweep(place, carry):
        values, low_flow = carry
        values_ahead = residual[place + 1, inner]
        pairs = [ahead[number, place, inner] for number in range(6)]
        flow_x = pairs[0] * values + pairs[1] * values_ahead
        flow_y = pairs[2] * values + pairs[3] * residual[place, above]
        under_y = ahead[2, place, below] * residual[place, below] + ahead[3, place, below] * values
        flow_z = pairs[4] * values + pairs[5] * roll_back(values, 1)
        change = (flow_x - low_flow) + (flow_y - under_y) + (flow_z - pltpu.roll(flow_z, 1, 1))
        store(place, state[place, inner] + (near * values - far * change))
        return values_ahead, flow_x

    if store is None:
        lax.fori_loop(0, total, second_sweep, (residual[0], zero), unroll=16)
    else:
        lax.fori_loop(0, total, inner_sweep, (residual[0, inner], zero[:rows]), unroll=16)


def bounds_of(packed):
    part = pl.ds(packed.shape[1] - 8, 8)
    bounds = packed[0, part]
    for entry in range(1, packed.shape[0]):
        bounds = jnp.maximum(bounds, packed[entry, part])
    return bounds


def first_kernel(rows, width, layers, info, rates, packed, *refs):
    def store(place, values):
        advanced[place] = values

    faces, (advanced, third, edge_one, edge_two), (state, spare, residual, ahead) = refs[:6], refs[6:10], refs[10:]
    total = state.shape[0] - 1
    zero = jnp.zeros(state.shape[1:], jnp.float32)
    state[total] = zero
    spare[total] = zero
    residual[total] = zero
    for place in range(total):
        state[place] = packed[place // layers, pl.ds(place % layers * width, width)]
    bounds = bounds_of(packed)
    for k in range(FINE):
        near, far = coefficients(bounds[k : k + 1])
        states = (state, spare) if k % 2 == 0 else (spare, state)
        step = (*states, residual, ahead, faces, packed, rates[pl.ds(k, 1)], near, far)
        if k < FINE - 1:
            one_step(total, width, layers, *step)
        else:
            one_step(total, width, layers, *step, rows, store)
        if k == FINE - 2:
            third[...] = states[1][:total, LOW : LOW + rows]
    edge = min(rows, LOW)
    low, high = advanced[:, :edge], advanced[:, rows - edge :]
    even = info[5] % 2 == 0
    edge_one[...] = jnp.where(even, high, low)
    edge_two[...] = jnp.where(even, low, high)


def second_kernel(rows, width, layers, info, rates, packed, passed, halo_one, halo_two, advanced, third, *refs):
    first = info[0] == 0

    def store(place, values):
        out[place // layers, 0, place % layers] = advanced[place]
        out[place // layers, 1, place % layers] = jnp.where(first, third[place], values)

    faces, out, (state, spare, residual, ahead) = refs[:6], refs[6], refs[7:]
    total = state.shape[0] - 1
    zero = jnp.zeros(state.shape[1:], jnp.float32)
    state[total] = zero
    spare[total] = zero
    residual[total] = zero
    swap = info[2] == 1
    below, above = halo_one[...], halo_two[...]
    low = jnp.where(swap, above, below)
    high = jnp.where(swap, below, above)
    state[:total, :LOW] = jnp.where(info[3] == 1, low, 0.0)
    state[:total, LOW : LOW + rows] = passed[...]
    state[:total, LOW + rows : 2 * LOW + rows] = jnp.where(info[4] == 1, high, 0.0)
    if width > 2 * LOW + rows:
        state[:total, 2 * LOW + rows :] = jnp.zeros((total, width - 2 * LOW - rows, state.shape[-1]), jnp.float32)
    bounds = bounds_of(packed)
    for k in range(FINE - 1):
        near, far = coefficients(bounds[k : k + 1])
        states = (state, spare) if k % 2 == 0 else (spare, state)
        step = (*states, residual, ahead, faces, packed, rates[pl.ds(k, 1)], near, far)
        if k < FINE - 2:
            one_step(total, width, layers, *step)
        else:
            one_step(total, width, layers, *step, rows, store)


def unpack_kernel(result, *refs):
    outs, sems = refs[:2], refs[2]
    count, rows = result.shape[0], result.shape[3]
    copies = []
    for number, out in enumerate(outs):
        for spot in range(count):
            target = out.at[0, :, pl.ds(slab_of(spot, count) * rows, rows)]
            copies.append(pltpu.make_async_copy(result.at[spot, number], target, sems.at[number, spot]))
    for copy in copies:
        copy.start()
    for copy in copies:
        copy.wait()


def swapped(array, sizes, partner, flip=0):
    copies, blocks, count = sizes
    pairs = []
    for c in range(copies):
        for t in range(blocks):
            for s in range(count):
                target = partner(t, s)
                if target is not None:
                    pairs.append(((c * blocks + t) * count + s, ((c ^ flip) * blocks + target[0]) * count + target[1]))
    return lax.ppermute(array, AXES, pairs)


def outer_partner(count):
    return lambda t, s: (t, ((s + 1) ^ 1) - 1) if 0 < s < count - 1 else (t ^ 1, s)


def halos(edge_one, edge_two, advanced, sizes, rows, slab):
    copies, blocks, count = sizes
    even = slab % 2 == 0
    below, above = slab > 0, slab < count - 1
    if rows >= LOW and blocks == 2 and count % 2 == 0:
        def partner(t, s):
            own = slab_of(s, count)
            return 1 - t, slab_of(((own + 1) ^ 1) - 1, count) if 0 < own < count - 1 else s

        one = swapped(edge_one, sizes, lambda t, s: (1 - t, s ^ 1))
        two = swapped(edge_two, sizes, partner)
        return one, two, even, below, above

    def shifted(values, by):
        return swapped(
            values, sizes, lambda t, s: (t + 1, s + by) if t + 1 < blocks and 0 <= s + by < count else None
        )

    reach = -(-LOW // rows)
    low = jnp.concatenate([shifted(advanced, by) for by in range(reach, 0, -1)], axis=1)[:, -LOW:]
    high = jnp.concatenate([shifted(advanced, -by) for by in range(1, reach + 1)], axis=1)[:, :LOW]
    return low, high, False, True, True


def shards(sizes, initial, source, diffusion, wind_field, buildings, strength):
    copies, blocks, count = sizes
    layers, depth, lanes = diffusion.shape
    total, rows = layers * count, depth // count
    width = -(-(rows + 2 * LOW) // 8) * 8
    block, place = lax.axis_index("tm"), lax.axis_index("space")
    params = pltpu.CompilerParams(vmem_limit_bytes=48 * 1024 * 1024)

    def struct(*shape):
        return jax.ShapeDtypeStruct(shape, jnp.float32)

    def call(kernel, outs, in_specs, name, *operands, **options):
        return pl.pallas_call(
            kernel,
            out_shape=outs,
            in_specs=in_specs,
            out_specs=[VMEM] * len(outs),
            name=name,
            **{"compiler_params": params, **options},
        )(*operands)

    half = block % 2
    lead = lax.axis_index("copy") % 2
    slab = slab_of(place, count)
    flags = [half, place, place > 0, place < count - 1, lead, slab]
    info = jnp.stack([jnp.asarray(flag).astype(jnp.int32) for flag in flags])
    field = struct(layers, depth, lanes)
    outer = struct(depth, lanes)
    hold = pltpu.VMEM((layers, depth, lanes), jnp.float32)
    anywhere = pl.BlockSpec(memory_space=pltpu.HBM)
    arrays = (initial, source, diffusion, wind_field, buildings, strength)
    masked, winds, state, forcing, edge_one, edge_two, rates = call(
        load_kernel,
        [field, struct(3, layers, depth, lanes), field, field, outer, outer, struct(8, lanes)],
        [SMEM] + [anywhere] * 6,
        "load",
        info,
        *(pltpu.with_memory_space_constraint(array, pltpu.HBM) for array in arrays),
        scratch_shapes=[
            hold,
            hold,
            pltpu.VMEM((layers, depth, lanes), source.dtype),
            pltpu.VMEM((layers, depth, lanes), jnp.int32),
            pltpu.SMEM(strength.shape, jnp.float32),
            pltpu.SemaphoreType.DMA((6,)),
        ],
    )
    same, across = call(
        functools.partial(pack_shared, rows, width),
        [struct(count // 2, layers, width, lanes)] * 2,
        [SMEM] + [VMEM] * 2,
        "pack_shared",
        info,
        masked,
        winds,
    )
    across = swapped(across, sizes, lambda t, s: (t, s ^ 1))
    edge_one = swapped(edge_one, sizes, lambda t, s: (t, s ^ 1))
    edge_two = swapped(edge_two, sizes, outer_partner(count))
    edges = jnp.stack([edge_one, edge_two])
    other_edges = swapped(edges, sizes, lambda t, s: (t ^ 1, s))
    (packed,) = call(
        functools.partial(bound_kernel, rows, width),
        [struct(count, 2 * layers * width + 8, lanes)],
        [SMEM] + [VMEM] * 7,
        "bounds",
        info,
        rates,
        edges,
        other_edges,
        masked,
        winds,
        state,
        forcing,
    )
    pieces = jnp.stack([same, across], axis=1)
    parts = [pieces[0]]
    for step in range(1, count // 2):
        parts.append(swapped(pieces[step], sizes, lambda t, s: (t, s ^ (2 * step))))
    *parts, _ = lax.optimization_barrier((*parts, packed))
    packed = lax.all_to_all(packed, "space", 0, 0, tiled=True)
    mine = jnp.concatenate(parts)
    beside = swapped(mine, sizes, lambda t, s: (t, s), 1)
    other = swapped(mine, sizes, lambda t, s: (t ^ 1, s))
    other_beside = swapped(beside, sizes, lambda t, s: (t ^ 1, s))
    faces = call(
        face_kernel,
        [struct(total, width, lanes)] * 6,
        [SMEM] + [VMEM] * 4,
        "faces",
        info,
        mine,
        beside,
        other,
        other_beside,
    )

    edge = min(rows, LOW)
    scratch = [
        pltpu.VMEM((total + 1, width, lanes), jnp.float32),
        pltpu.VMEM((total + 1, width, lanes), jnp.float32),
        pltpu.VMEM((total + 1, width, lanes), jnp.float32),
        pltpu.VMEM((6, total, width, lanes), jnp.float32),
    ]
    advanced, third, edge_one, edge_two = pl.pallas_call(
        functools.partial(first_kernel, rows, width, layers),
        out_shape=[struct(total, rows, lanes)] * 2 + [struct(total, edge, lanes)] * 2,
        in_specs=[SMEM] + [VMEM] * 8,
        out_specs=[VMEM] * 4,
        scratch_shapes=scratch,
        compiler_params=params,
        name="four_steps",
    )(info, rates, packed, *faces)

    if blocks == 2:
        own = swapped(advanced, sizes, lambda t, s: (1 - t, s))
    else:
        own = swapped(advanced, sizes, lambda t, s: (t + 1, s) if t + 1 < blocks else None)
    one, two, swap, below, above = halos(edge_one, edge_two, advanced, sizes, rows, slab)
    flags = [block, place, swap, below, above]
    info = jnp.stack([jnp.asarray(flag).astype(jnp.int32) for flag in flags])
    result = pl.pallas_call(
        functools.partial(second_kernel, rows, width, layers),
        out_shape=struct(count, 2, layers, rows, lanes),
        in_specs=[SMEM] + [VMEM] * 13,
        out_specs=VMEM,
        scratch_shapes=scratch,
        compiler_params=params,
        name="three_steps",
    )(info, rates, packed, own, one, two, advanced, third, *faces)
    result = lax.all_to_all(result, "space", 0, 0, tiled=True)
    if rows % 8:
        result = result.transpose(1, 2, 0, 3, 4).reshape(2, 1, layers, depth, lanes)
        return result[0], result[1]
    return tuple(
        pl.pallas_call(
            unpack_kernel,
            out_shape=[struct(1, layers, depth, lanes)] * 2,
            in_specs=[VMEM],
            out_specs=[pl.BlockSpec(memory_space=pl.ANY)] * 2,
            scratch_shapes=[pltpu.SemaphoreType.DMA((2, count))],
            compiler_params=params,
            name="unpack",
        )(result)
    )


def solution(mesh):
    sizes = tuple(mesh.shape[axis] for axis in AXES)
    in_specs = (
        P(("copy", "tm"), "space", None, None),
        P(("copy", "tm"), "space", None, None),
        P("space", None, None),
        P(None, "space", None, None),
        P("space", None, None),
        P("tm", None),
    )
    out_specs = (P(("copy", "tm"), "space", None, None), P(("copy", "tm"), "space", None, None))
    return jax.shard_map(
        functools.partial(shards, sizes), mesh=mesh, in_specs=in_specs, out_specs=out_specs, check_vma=False
    )
```

```python
import functools

import jax
import jax.numpy as jnp
from jax import lax
from jax.experimental import pallas as pl
from jax.experimental.pallas import tpu as pltpu
from jax.sharding import PartitionSpec as P

FINE = 4
LOW = 2 * FINE
lower_bound = 0.5
AXES = ("copy", "tm", "space")
VMEM = pl.BlockSpec(memory_space=pltpu.VMEM)
SMEM = pl.BlockSpec(memory_space=pltpu.SMEM)


def slab_of(place, count):
    return place ^ (place // 2 % 2) if count == 8 else place


def windows(values, place, rows, width):
    total, lanes = values.shape
    start = rows * place - LOW
    first, last = max(start, 0), min(start + width, total)
    parts = []
    if first > start:
        parts.append(jnp.zeros((first - start, lanes), values.dtype))
    parts.append(values[first:last])
    if last < start + width:
        parts.append(jnp.zeros((start + width - last, lanes), values.dtype))
    return jnp.concatenate(parts, axis=0) if len(parts) > 1 else parts[0]


def load_kernel(info, initial, source, diffusion, wind, buildings, strength, *rest):
    masked, winds, state, forcing, edge_one, edge_two, rates, fresh, early, late, solid, steps, sems = rest
    pairs = (
        (diffusion, fresh),
        (buildings, solid),
        (wind, winds),
        (initial.at[0], early),
        (source.at[0], late),
        (strength, steps),
    )
    copies = [pltpu.make_async_copy(*pair, sems.at[number]) for number, pair in enumerate(pairs)]
    for copy in copies:
        copy.start()
    for copy in copies[:3]:
        copy.wait()
    opened = (1 - solid[...]).astype(jnp.float32)
    masked[...] = fresh[...] * opened
    first, even = info[0] == 0, info[1] % 2 == 0
    last = masked.shape[0] - 1
    low = jnp.where(first, masked[0], winds[0, 0])
    high = jnp.where(first, masked[last], winds[0, last])
    edge_one[...] = jnp.where(even, high, low)
    edge_two[...] = jnp.where(even, low, high)
    for copy in copies[3:]:
        copy.wait()
    state[...] = early[...] * opened
    forcing[...] = late[...].astype(jnp.float32) * opened
    place = lax.broadcasted_iota(jnp.int32, rates.shape, 0)
    table = jnp.zeros(rates.shape, jnp.float32)
    for k in range(FINE):
        table = jnp.where(place == k, steps[0, k], table)
    rates[...] = table


def pack_shared(rows, width, info, masked, wind, same, across):
    first, spot, lead = info[0] == 0, info[1], info[4] == 0
    half = same.shape[0]
    swap = spot % 2 == 1
    for layer in range(masked.shape[0]):
        field = jnp.where(
            first,
            jnp.where(lead, masked[layer], wind[0, layer]),
            jnp.where(lead, wind[1, layer], wind[2, layer]),
        )
        for place in range(half):
            even = windows(field, slab_of(2 * place, 2 * half), rows, width)
            odd = windows(field, slab_of(2 * place + 1, 2 * half), rows, width)
            same[place ^ (spot // 2), layer] = jnp.where(swap, odd, even)
            across[place ^ (spot // 2), layer] = jnp.where(swap, even, odd)


def pack_own(rows, width, state, forcing, packed):
    layers = state.shape[0]
    for layer in range(layers):
        for spot in range(packed.shape[0]):
            packed[spot, pl.ds(layer * width, width)] = windows(state[layer], slab_of(spot, packed.shape[0]), rows, width)
            packed[spot, pl.ds((layers + layer) * width, width)] = windows(forcing[layer], slab_of(spot, packed.shape[0]), rows, width)


def bound_kernel(rows, width, info, rates, mine, other, masked, wind, state, forcing, out, bulk, tail, sems):
    size = bulk.shape[1]
    pack_own(rows, width, state, forcing, bulk)
    copies = [
        pltpu.make_async_copy(bulk, out.at[:, pl.ds(0, size)], sems.at[0]),
        pltpu.make_async_copy(tail, out.at[:, pl.ds(size, tail.shape[1])], sems.at[1]),
    ]
    copies[0].start()
    first, even = info[0] == 0, info[1] % 2 == 0
    here, there = (mine[0], mine[1]), (other[0], other[1])

    def sides(one, two, keep):
        above, below = jnp.where(even, one, two), jnp.where(even, two, one)
        if keep:
            below, above = jnp.where(info[2] == 1, below, 0.0), jnp.where(info[3] == 1, above, 0.0)
        return below, above

    masked_sides = sides(jnp.where(first, here[0], there[0]), jnp.where(first, here[1], there[1]), True)
    wind_sides = sides(jnp.where(first, there[0], here[0]), jnp.where(first, there[1], here[1]), False)
    layers, depth, lanes = masked.shape
    chunk = 16 if depth % 16 == 0 else depth
    row = lax.broadcasted_iota(jnp.int32, (chunk, lanes), 0)
    inner_lane = lax.broadcasted_iota(jnp.int32, (chunk, lanes), 1) < lanes - 1

    def face(here, ahead, wind_here, wind_ahead):
        both = jnp.where((here > 0.0) & (ahead > 0.0), 1.0, 0.0)
        return jnp.sqrt(here * ahead), jnp.abs(0.5 * (wind_here + wind_ahead) * both)

    peaks = [jnp.zeros((8, lanes), jnp.float32)] * FINE
    edge = [[jnp.zeros((1, lanes), jnp.float32)] * 2 for _ in range(layers)]
    for start in range(0, depth, chunk):
        part = pl.ds(start, chunk)
        fields = [masked_sides[0][start : start + chunk]]
        fields += [masked[layer, part] for layer in range(layers)]
        fields += [masked_sides[1][start : start + chunk]]
        winds = [wind_sides[0][start : start + chunk]]
        winds += [wind[0, layer, part] for layer in range(layers)]
        winds += [wind_sides[1][start : start + chunk]]
        below = face(fields[0], fields[1], winds[0], winds[1])
        for layer in range(layers):
            field = fields[layer + 1]
            above = face(field, fields[layer + 2], winds[layer + 1], winds[layer + 2])
            sums = [above[0] + below[0], above[1] + below[1]]
            below = above
            flow = wind[1, layer, part]
            if start + chunk < depth:
                following = pl.ds(start + 1, chunk)
                pair = face(field, masked[layer, following], flow, wind[1, layer, following])
            else:
                pair = face(field, roll_back(field, 0), flow, roll_back(flow, 0))
                pair = [jnp.where(row < chunk - 1, value, 0.0) for value in pair]
            for number in range(2):
                value = pair[number]
                lower = jnp.where(row == 0, edge[layer][number], pltpu.roll(value, 1, 0))
                edge[layer][number] = value[chunk - 1 : chunk]
                sums[number] = sums[number] + value + lower
            flow = wind[2, layer, part]
            pair = face(field, roll_back(field, 1), flow, roll_back(flow, 1))
            for number in range(2):
                value = jnp.where(inner_lane, pair[number], 0.0)
                sums[number] = sums[number] + value + pltpu.roll(value, 1, 1)
            still = 1.0 + 2.0 * sums[0]
            for k in range(FINE):
                bound = still + rates[pl.ds(k, 1)] * sums[1]
                for first_row in range(0, chunk, 8):
                    peaks[k] = jnp.maximum(peaks[k], bound[first_row : first_row + 8])
    bounds = jnp.zeros((8, lanes), jnp.float32)
    place = lax.broadcasted_iota(jnp.int32, (8, lanes), 0)
    for k in range(FINE):
        bounds = jnp.where(place == k, jnp.max(peaks[k]), bounds)
    tail[...] = jnp.broadcast_to(bounds, tail.shape)
    copies[1].start()
    for copy in copies:
        copy.wait()


def roll_back(values, axis):
    return pltpu.roll(values, values.shape[axis] - 1, axis)


def face_kernel(info, mine, beside, other, other_beside, *faces):
    count, layers, width, lanes = mine.shape
    total = count * layers
    first, own, lead = info[0] == 0, info[1], info[4] == 0
    row = lax.broadcasted_iota(jnp.int32, (width, lanes), 0)
    lane = lax.broadcasted_iota(jnp.int32, (width, lanes), 1)
    inner_row = row < width - 1
    inner_lane = lane < lanes - 1
    zero = jnp.zeros((width, lanes), jnp.float32)

    def fields(place):
        spot, layer = (place // layers) ^ own, place % layers

        def ordered(one, two):
            one, two = one[spot, layer], two[spot, layer]
            return jnp.where(lead, one, two), jnp.where(lead, two, one)

        here, there = ordered(mine, beside), ordered(other, other_beside)
        masked = jnp.where(first, here[0], there[0])
        wind_x = jnp.where(first, here[1], there[1])
        wind_y = jnp.where(first, there[0], here[0])
        wind_z = jnp.where(first, there[1], here[1])
        return masked, wind_x, wind_y, wind_z

    def body(place, carry):
        masked, wind_x, wind_y, wind_z = carry
        following = fields(jnp.minimum(place + 1, total - 1))
        next_masked = jnp.where(place < total - 1, following[0], zero)
        opened = jnp.where(masked > 0.0, 1.0, 0.0)

        def face(masked_ahead, wind_here, wind_ahead, keep):
            conduct = jnp.sqrt(masked * masked_ahead)
            speed = 0.5 * (wind_here + wind_ahead) * opened * jnp.where(masked_ahead > 0.0, 1.0, 0.0)
            if keep is not None:
                conduct, speed = jnp.where(keep, conduct, 0.0), jnp.where(keep, speed, 0.0)
            return conduct, speed

        along_x = face(next_masked, wind_x, following[1], None)
        along_y = face(roll_back(masked, 0), wind_y, roll_back(wind_y, 0), inner_row)
        along_z = face(roll_back(masked, 1), wind_z, roll_back(wind_z, 1), inner_lane)
        for number, value in enumerate(along_x + along_y + along_z):
            faces[number][place] = value
        return next_masked, *following[1:]

    lax.fori_loop(0, total, body, fields(0), unroll=8)


def coefficients(bound):
    theta = (bound + lower_bound) * 0.5
    delta = (bound - lower_bound) * 0.5
    sigma = theta / delta
    rho_one = 1.0 / sigma
    rho_two = 1.0 / (2.0 * sigma - rho_one)
    beta = 2.0 * rho_two / (delta * theta)
    alpha = (1.0 + rho_one * rho_two) / theta + 2.0 * rho_two / delta
    return alpha - beta, beta


def one_step(total, width, layers, state, result, residual, ahead, faces, packed, rate, near, far, rows=0, store=None):
    lanes = state.shape[-1]
    zero = jnp.zeros((width, lanes), jnp.float32)

    def difference(place, values, values_ahead, low_flow, pairs):
        flow_x = pairs[0] * values + pairs[1] * values_ahead
        flow_y = pairs[2] * values + pairs[3] * roll_back(values, 0)
        flow_z = pairs[4] * values + pairs[5] * roll_back(values, 1)
        change = (flow_x - low_flow) + (flow_y - pltpu.roll(flow_y, 1, 0)) + (flow_z - pltpu.roll(flow_z, 1, 1))
        return change, flow_x

    def first_sweep(place, carry):
        values, low_flow = carry
        values_ahead = state[place + 1]
        pairs = []
        for dim in range(3):
            conduct, speed = faces[2 * dim][place], faces[2 * dim + 1][place]
            speed = rate * speed
            pairs.append(conduct + jnp.maximum(speed, 0.0))
            pairs.append(jnp.minimum(speed, 0.0) - conduct)
        for number in range(6):
            ahead[number, place] = pairs[number]
        change, low_flow = difference(place, values, values_ahead, low_flow, pairs)
        spot, layer = place // layers, place % layers
        offset = pl.multiple_of((layers + layer) * width, 8)
        residual[place] = packed[spot, pl.ds(offset, width)] - change
        return values_ahead, low_flow

    def second_sweep(place, carry):
        values, low_flow = carry
        values_ahead = residual[place + 1]
        pairs = [ahead[number, place] for number in range(6)]
        change, low_flow = difference(place, values, values_ahead, low_flow, pairs)
        result[place] = state[place] + (near * values - far * change)
        return values_ahead, low_flow

    lax.fori_loop(0, total, first_sweep, (state[0], zero), unroll=8)
    inner, below, above = pl.ds(LOW, rows), pl.ds(LOW - 1, rows), pl.ds(LOW + 1, rows)

    def inner_sweep(place, carry):
        values, low_flow = carry
        values_ahead = residual[place + 1, inner]
        pairs = [ahead[number, place, inner] for number in range(6)]
        flow_x = pairs[0] * values + pairs[1] * values_ahead
        flow_y = pairs[2] * values + pairs[3] * residual[place, above]
        under_y = ahead[2, place, below] * residual[place, below] + ahead[3, place, below] * values
        flow_z = pairs[4] * values + pairs[5] * roll_back(values, 1)
        change = (flow_x - low_flow) + (flow_y - under_y) + (flow_z - pltpu.roll(flow_z, 1, 1))
        store(place, state[place, inner] + (near * values - far * change))
        return values_ahead, flow_x

    if store is None:
        lax.fori_loop(0, total, second_sweep, (residual[0], zero), unroll=16)
    else:
        lax.fori_loop(0, total, inner_sweep, (residual[0, inner], zero[:rows]), unroll=16)


def bounds_of(packed):
    part = pl.ds(packed.shape[1] - 8, 8)
    bounds = packed[0, part]
    for entry in range(1, packed.shape[0]):
        bounds = jnp.maximum(bounds, packed[entry, part])
    return bounds


def first_kernel(rows, width, layers, info, rates, packed, *refs):
    def store(place, values):
        advanced[place] = values

    faces, (advanced, third, edge_one, edge_two), (state, spare, residual, ahead) = refs[:6], refs[6:10], refs[10:]
    total = state.shape[0] - 1
    zero = jnp.zeros(state.shape[1:], jnp.float32)
    state[total] = zero
    spare[total] = zero
    residual[total] = zero
    for place in range(total):
        state[place] = packed[place // layers, pl.ds(place % layers * width, width)]
    bounds = bounds_of(packed)
    for k in range(FINE):
        near, far = coefficients(bounds[k : k + 1])
        states = (state, spare) if k % 2 == 0 else (spare, state)
        step = (*states, residual, ahead, faces, packed, rates[pl.ds(k, 1)], near, far)
        if k < FINE - 1:
            one_step(total, width, layers, *step)
        else:
            one_step(total, width, layers, *step, rows, store)
        if k == FINE - 2:
            third[...] = states[1][:total, LOW : LOW + rows]
    edge = min(rows, LOW)
    low, high = advanced[:, :edge], advanced[:, rows - edge :]
    even = info[5] % 2 == 0
    edge_one[...] = jnp.where(even, high, low)
    edge_two[...] = jnp.where(even, low, high)


def second_kernel(rows, width, layers, info, rates, packed, passed, halo_one, halo_two, advanced, third, *refs):
    first = info[0] == 0

    def store(place, values):
        out[place // layers, 0, place % layers] = advanced[place]
        out[place // layers, 1, place % layers] = jnp.where(first, third[place], values)

    faces, out, (state, spare, residual, ahead) = refs[:6], refs[6], refs[7:]
    total = state.shape[0] - 1
    zero = jnp.zeros(state.shape[1:], jnp.float32)
    state[total] = zero
    spare[total] = zero
    residual[total] = zero
    swap = info[2] == 1
    below, above = halo_one[...], halo_two[...]
    low = jnp.where(swap, above, below)
    high = jnp.where(swap, below, above)
    state[:total, :LOW] = jnp.where(info[3] == 1, low, 0.0)
    state[:total, LOW : LOW + rows] = passed[...]
    state[:total, LOW + rows : 2 * LOW + rows] = jnp.where(info[4] == 1, high, 0.0)
    if width > 2 * LOW + rows:
        state[:total, 2 * LOW + rows :] = jnp.zeros((total, width - 2 * LOW - rows, state.shape[-1]), jnp.float32)
    bounds = bounds_of(packed)
    for k in range(FINE - 1):
        near, far = coefficients(bounds[k : k + 1])
        states = (state, spare) if k % 2 == 0 else (spare, state)
        step = (*states, residual, ahead, faces, packed, rates[pl.ds(k, 1)], near, far)
        if k < FINE - 2:
            one_step(total, width, layers, *step)
        else:
            one_step(total, width, layers, *step, rows, store)


def unpack_kernel(result, *refs):
    outs, sems = refs[:2], refs[2]
    count, rows = result.shape[0], result.shape[3]
    copies = []
    for number, out in enumerate(outs):
        for spot in range(count):
            target = out.at[0, :, pl.ds(slab_of(spot, count) * rows, rows)]
            copies.append(pltpu.make_async_copy(result.at[spot, number], target, sems.at[number, spot]))
    for copy in copies:
        copy.start()
    for copy in copies:
        copy.wait()


def swapped(array, sizes, partner, flip=0):
    copies, blocks, count = sizes
    pairs = []
    for c in range(copies):
        for t in range(blocks):
            for s in range(count):
                target = partner(t, s)
                if target is not None:
                    pairs.append(((c * blocks + t) * count + s, ((c ^ flip) * blocks + target[0]) * count + target[1]))
    return lax.ppermute(array, AXES, pairs)


def outer_partner(count):
    return lambda t, s: (t, ((s + 1) ^ 1) - 1) if 0 < s < count - 1 else (t ^ 1, s)


def halos(edge_one, edge_two, advanced, sizes, rows, slab):
    copies, blocks, count = sizes
    even = slab % 2 == 0
    below, above = slab > 0, slab < count - 1
    if rows >= LOW and blocks == 2 and count % 2 == 0:
        def partner(t, s):
            own = slab_of(s, count)
            return 1 - t, slab_of(((own + 1) ^ 1) - 1, count) if 0 < own < count - 1 else s

        one = swapped(edge_one, sizes, lambda t, s: (1 - t, s ^ 1))
        two = swapped(edge_two, sizes, partner)
        return one, two, even, below, above

    def shifted(values, by):
        return swapped(
            values, sizes, lambda t, s: (t + 1, s + by) if t + 1 < blocks and 0 <= s + by < count else None
        )

    reach = -(-LOW // rows)
    low = jnp.concatenate([shifted(advanced, by) for by in range(reach, 0, -1)], axis=1)[:, -LOW:]
    high = jnp.concatenate([shifted(advanced, -by) for by in range(1, reach + 1)], axis=1)[:, :LOW]
    return low, high, False, True, True


def shards(sizes, initial, source, diffusion, wind_field, buildings, strength):
    copies, blocks, count = sizes
    layers, depth, lanes = diffusion.shape
    total, rows = layers * count, depth // count
    width = -(-(rows + 2 * LOW) // 8) * 8
    block, place = lax.axis_index("tm"), lax.axis_index("space")
    params = pltpu.CompilerParams(vmem_limit_bytes=48 * 1024 * 1024)

    def struct(*shape):
        return jax.ShapeDtypeStruct(shape, jnp.float32)

    def call(kernel, outs, in_specs, name, *operands, **options):
        return pl.pallas_call(
            kernel,
            out_shape=outs,
            in_specs=in_specs,
            out_specs=[VMEM] * len(outs),
            name=name,
            **{"compiler_params": params, **options},
        )(*operands)

    half = block % 2
    lead = lax.axis_index("copy") % 2
    slab = slab_of(place, count)
    flags = [half, place, place > 0, place < count - 1, lead, slab]
    info = jnp.stack([jnp.asarray(flag).astype(jnp.int32) for flag in flags])
    field = struct(layers, depth, lanes)
    outer = struct(depth, lanes)
    hold = pltpu.VMEM((layers, depth, lanes), jnp.float32)
    anywhere = pl.BlockSpec(memory_space=pltpu.HBM)
    arrays = (initial, source, diffusion, wind_field, buildings, strength)
    masked, winds, state, forcing, edge_one, edge_two, rates = call(
        load_kernel,
        [field, struct(3, layers, depth, lanes), field, field, outer, outer, struct(8, lanes)],
        [SMEM] + [anywhere] * 6,
        "load",
        info,
        *(pltpu.with_memory_space_constraint(array, pltpu.HBM) for array in arrays),
        scratch_shapes=[
            hold,
            hold,
            pltpu.VMEM((layers, depth, lanes), source.dtype),
            pltpu.VMEM((layers, depth, lanes), jnp.int32),
            pltpu.SMEM(strength.shape, jnp.float32),
            pltpu.SemaphoreType.DMA((6,)),
        ],
    )
    same, across = call(
        functools.partial(pack_shared, rows, width),
        [struct(count // 2, layers, width, lanes)] * 2,
        [SMEM] + [VMEM] * 2,
        "pack_shared",
        info,
        masked,
        winds,
    )
    across = swapped(across, sizes, lambda t, s: (t, s ^ 1))
    edge_one = swapped(edge_one, sizes, lambda t, s: (t, s ^ 1))
    edge_two = swapped(edge_two, sizes, outer_partner(count))
    edges = jnp.stack([edge_one, edge_two])
    other_edges = swapped(edges, sizes, lambda t, s: (t ^ 1, s))
    size = 2 * layers * width
    packed = pl.pallas_call(
        functools.partial(bound_kernel, rows, width),
        out_shape=struct(count, size + 8, lanes),
        in_specs=[SMEM] + [VMEM] * 7,
        out_specs=pl.BlockSpec(memory_space=pl.ANY),
        scratch_shapes=[
            pltpu.VMEM((count, size, lanes), jnp.float32),
            pltpu.VMEM((count, 8, lanes), jnp.float32),
            pltpu.SemaphoreType.DMA((2,)),
        ],
        compiler_params=params,
        name="bounds",
    )(info, rates, edges, other_edges, masked, winds, state, forcing)
    pieces = jnp.stack([same, across], axis=1)
    parts = [pieces[0]]
    for step in range(1, count // 2):
        parts.append(swapped(pieces[step], sizes, lambda t, s: (t, s ^ (2 * step))))
    *parts, _ = lax.optimization_barrier((*parts, packed))
    packed = lax.all_to_all(packed, "space", 0, 0, tiled=True)
    mine = jnp.concatenate(parts)
    beside = swapped(mine, sizes, lambda t, s: (t, s), 1)
    other = swapped(mine, sizes, lambda t, s: (t ^ 1, s))
    other_beside = swapped(beside, sizes, lambda t, s: (t ^ 1, s))
    faces = call(
        face_kernel,
        [struct(total, width, lanes)] * 6,
        [SMEM] + [VMEM] * 4,
        "faces",
        info,
        mine,
        beside,
        other,
        other_beside,
    )

    edge = min(rows, LOW)
    scratch = [
        pltpu.VMEM((total + 1, width, lanes), jnp.float32),
        pltpu.VMEM((total + 1, width, lanes), jnp.float32),
        pltpu.VMEM((total + 1, width, lanes), jnp.float32),
        pltpu.VMEM((6, total, width, lanes), jnp.float32),
    ]
    advanced, third, edge_one, edge_two = pl.pallas_call(
        functools.partial(first_kernel, rows, width, layers),
        out_shape=[struct(total, rows, lanes)] * 2 + [struct(total, edge, lanes)] * 2,
        in_specs=[SMEM] + [VMEM] * 8,
        out_specs=[VMEM] * 4,
        scratch_shapes=scratch,
        compiler_params=params,
        name="four_steps",
    )(info, rates, packed, *faces)

    if blocks == 2:
        own = swapped(advanced, sizes, lambda t, s: (1 - t, s))
    else:
        own = swapped(advanced, sizes, lambda t, s: (t + 1, s) if t + 1 < blocks else None)
    one, two, swap, below, above = halos(edge_one, edge_two, advanced, sizes, rows, slab)
    flags = [block, place, swap, below, above]
    info = jnp.stack([jnp.asarray(flag).astype(jnp.int32) for flag in flags])
    result = pl.pallas_call(
        functools.partial(second_kernel, rows, width, layers),
        out_shape=struct(count, 2, layers, rows, lanes),
        in_specs=[SMEM] + [VMEM] * 13,
        out_specs=VMEM,
        scratch_shapes=scratch,
        compiler_params=params,
        name="three_steps",
    )(info, rates, packed, own, one, two, advanced, third, *faces)
    result = lax.all_to_all(result, "space", 0, 0, tiled=True)
    if rows % 8:
        result = result.transpose(1, 2, 0, 3, 4).reshape(2, 1, layers, depth, lanes)
        return result[0], result[1]
    return tuple(
        pl.pallas_call(
            unpack_kernel,
            out_shape=[struct(1, layers, depth, lanes)] * 2,
            in_specs=[VMEM],
            out_specs=[pl.BlockSpec(memory_space=pl.ANY)] * 2,
            scratch_shapes=[pltpu.SemaphoreType.DMA((2, count))],
            compiler_params=params,
            name="unpack",
        )(result)
    )


def solution(mesh):
    sizes = tuple(mesh.shape[axis] for axis in AXES)
    in_specs = (
        P(("copy", "tm"), "space", None, None),
        P(("copy", "tm"), "space", None, None),
        P("space", None, None),
        P(None, "space", None, None),
        P("space", None, None),
        P("tm", None),
    )
    out_specs = (P(("copy", "tm"), "space", None, None), P(("copy", "tm"), "space", None, None))
    return jax.shard_map(
        functools.partial(shards, sizes), mesh=mesh, in_specs=in_specs, out_specs=out_specs, check_vma=False
    )
```

```python
import functools

import jax
import jax.numpy as jnp
from jax import lax
from jax.experimental import pallas as pl
from jax.experimental.pallas import tpu as pltpu
from jax.sharding import PartitionSpec as P

FINE = 4
LOW = 2 * FINE
lower_bound = 0.5
AXES = ("copy", "tm", "space")
VMEM = pl.BlockSpec(memory_space=pltpu.VMEM)
SMEM = pl.BlockSpec(memory_space=pltpu.SMEM)


def slab_of(place, count):
    return place ^ (place // 2 % 2) if count == 8 else place


def windows(values, place, rows, width):
    total, lanes = values.shape
    start = rows * place - LOW
    first, last = max(start, 0), min(start + width, total)
    parts = []
    if first > start:
        parts.append(jnp.zeros((first - start, lanes), values.dtype))
    parts.append(values[first:last])
    if last < start + width:
        parts.append(jnp.zeros((start + width - last, lanes), values.dtype))
    return jnp.concatenate(parts, axis=0) if len(parts) > 1 else parts[0]


def load_kernel(rows, width, info, initial, source, diffusion, wind, buildings, strength, *rest):
    masked, winds, state, forcing, edge_one, edge_two, rates, same, across, fresh, early, late, solid, steps, sems = rest
    pairs = (
        (diffusion, fresh),
        (buildings, solid),
        (wind, winds),
        (initial.at[0], early),
        (source.at[0], late),
        (strength, steps),
    )
    copies = [pltpu.make_async_copy(*pair, sems.at[number]) for number, pair in enumerate(pairs)]
    for copy in copies:
        copy.start()
    for copy in copies[:3]:
        copy.wait()
    opened = (1 - solid[...]).astype(jnp.float32)
    masked[...] = fresh[...] * opened
    first, even = info[0] == 0, info[1] % 2 == 0
    last = masked.shape[0] - 1
    low = jnp.where(first, masked[0], winds[0, 0])
    high = jnp.where(first, masked[last], winds[0, last])
    edge_one[...] = jnp.where(even, high, low)
    edge_two[...] = jnp.where(even, low, high)
    pack_shared(rows, width, info, masked, winds, same, across)
    for copy in copies[3:]:
        copy.wait()
    state[...] = early[...] * opened
    forcing[...] = late[...].astype(jnp.float32) * opened
    place = lax.broadcasted_iota(jnp.int32, rates.shape, 0)
    table = jnp.zeros(rates.shape, jnp.float32)
    for k in range(FINE):
        table = jnp.where(place == k, steps[0, k], table)
    rates[...] = table


def pack_shared(rows, width, info, masked, wind, same, across):
    first, spot, lead = info[0] == 0, info[1], info[4] == 0
    half = same.shape[0]
    swap = spot % 2 == 1
    for layer in range(masked.shape[0]):
        field = jnp.where(
            first,
            jnp.where(lead, masked[layer], wind[0, layer]),
            jnp.where(lead, wind[1, layer], wind[2, layer]),
        )
        for place in range(half):
            even = windows(field, slab_of(2 * place, 2 * half), rows, width)
            odd = windows(field, slab_of(2 * place + 1, 2 * half), rows, width)
            entry = place ^ (spot // 2)
            same[entry, layer] = jnp.where(swap, odd, even)
            across[entry, layer] = jnp.where(swap, even, odd)


def pack_own(rows, width, state, forcing, packed):
    layers = state.shape[0]
    for layer in range(layers):
        for spot in range(packed.shape[0]):
            packed[spot, pl.ds(layer * width, width)] = windows(state[layer], slab_of(spot, packed.shape[0]), rows, width)
            packed[spot, pl.ds((layers + layer) * width, width)] = windows(forcing[layer], slab_of(spot, packed.shape[0]), rows, width)


def bound_kernel(rows, width, info, rates, mine, other, masked, wind, state, forcing, out):
    first, even = info[0] == 0, info[1] % 2 == 0
    here, there = (mine[0], mine[1]), (other[0], other[1])

    def sides(one, two, keep):
        above, below = jnp.where(even, one, two), jnp.where(even, two, one)
        if keep:
            below, above = jnp.where(info[2] == 1, below, 0.0), jnp.where(info[3] == 1, above, 0.0)
        return below, above

    masked_sides = sides(jnp.where(first, here[0], there[0]), jnp.where(first, here[1], there[1]), True)
    wind_sides = sides(jnp.where(first, there[0], here[0]), jnp.where(first, there[1], here[1]), False)
    layers, depth, lanes = masked.shape
    chunk = 32 if depth % 32 == 0 else depth
    row = lax.broadcasted_iota(jnp.int32, (chunk, lanes), 0)
    inner_lane = lax.broadcasted_iota(jnp.int32, (chunk, lanes), 1) < lanes - 1

    def face(here, ahead, wind_here, wind_ahead):
        both = jnp.where((here > 0.0) & (ahead > 0.0), 1.0, 0.0)
        return jnp.sqrt(here * ahead), jnp.abs(0.5 * (wind_here + wind_ahead) * both)

    peaks = [jnp.zeros((chunk, lanes), jnp.float32)] * FINE
    edge = [[jnp.zeros((1, lanes), jnp.float32)] * 2 for _ in range(layers)]
    for start in range(0, depth, chunk):
        part = pl.ds(start, chunk)
        fields = [masked_sides[0][start : start + chunk]]
        fields += [masked[layer, part] for layer in range(layers)]
        fields += [masked_sides[1][start : start + chunk]]
        winds = [wind_sides[0][start : start + chunk]]
        winds += [wind[0, layer, part] for layer in range(layers)]
        winds += [wind_sides[1][start : start + chunk]]
        below = face(fields[0], fields[1], winds[0], winds[1])
        for layer in range(layers):
            field = fields[layer + 1]
            above = face(field, fields[layer + 2], winds[layer + 1], winds[layer + 2])
            sums = [above[0] + below[0], above[1] + below[1]]
            below = above
            flow = wind[1, layer, part]
            if start + chunk < depth:
                following = pl.ds(start + 1, chunk)
                pair = face(field, masked[layer, following], flow, wind[1, layer, following])
            else:
                pair = face(field, roll_back(field, 0), flow, roll_back(flow, 0))
                pair = [jnp.where(row < chunk - 1, value, 0.0) for value in pair]
            for number in range(2):
                value = pair[number]
                lower = jnp.where(row == 0, edge[layer][number], pltpu.roll(value, 1, 0))
                edge[layer][number] = value[chunk - 1 : chunk]
                sums[number] = sums[number] + value + lower
            flow = wind[2, layer, part]
            pair = face(field, roll_back(field, 1), flow, roll_back(flow, 1))
            for number in range(2):
                value = jnp.where(inner_lane, pair[number], 0.0)
                sums[number] = sums[number] + value + pltpu.roll(value, 1, 1)
            still = 1.0 + 2.0 * sums[0]
            for k in range(FINE):
                peaks[k] = jnp.maximum(peaks[k], still + rates[pl.ds(k, 1)] * sums[1])
    bounds = jnp.zeros((8, lanes), jnp.float32)
    place = lax.broadcasted_iota(jnp.int32, (8, lanes), 0)
    for k in range(FINE):
        bounds = jnp.where(place == k, jnp.max(peaks[k]), bounds)
    pack_own(rows, width, state, forcing, out)
    start = out.shape[1] - 8
    for spot in range(out.shape[0]):
        out[spot, pl.ds(start, 8)] = bounds


def roll_back(values, axis):
    return pltpu.roll(values, values.shape[axis] - 1, axis)


def face_kernel(info, mine, beside, other, other_beside, *faces):
    count, layers, width, lanes = mine.shape
    total = count * layers
    first, own, lead = info[0] == 0, info[1], info[4] == 0
    row = lax.broadcasted_iota(jnp.int32, (width, lanes), 0)
    lane = lax.broadcasted_iota(jnp.int32, (width, lanes), 1)
    inner_row = row < width - 1
    inner_lane = lane < lanes - 1
    zero = jnp.zeros((width, lanes), jnp.float32)

    def fields(place):
        spot, layer = (place // layers) ^ own, place % layers

        def ordered(one, two):
            one, two = one[spot, layer], two[spot, layer]
            return jnp.where(lead, one, two), jnp.where(lead, two, one)

        here, there = ordered(mine, beside), ordered(other, other_beside)
        masked = jnp.where(first, here[0], there[0])
        wind_x = jnp.where(first, here[1], there[1])
        wind_y = jnp.where(first, there[0], here[0])
        wind_z = jnp.where(first, there[1], here[1])
        return masked, wind_x, wind_y, wind_z

    def body(place, carry):
        masked, wind_x, wind_y, wind_z = carry
        following = fields(jnp.minimum(place + 1, total - 1))
        next_masked = jnp.where(place < total - 1, following[0], zero)
        opened = jnp.where(masked > 0.0, 1.0, 0.0)

        def face(masked_ahead, wind_here, wind_ahead, keep):
            conduct = jnp.sqrt(masked * masked_ahead)
            speed = 0.5 * (wind_here + wind_ahead) * opened * jnp.where(masked_ahead > 0.0, 1.0, 0.0)
            if keep is not None:
                conduct, speed = jnp.where(keep, conduct, 0.0), jnp.where(keep, speed, 0.0)
            return conduct, speed

        along_x = face(next_masked, wind_x, following[1], None)
        along_y = face(roll_back(masked, 0), wind_y, roll_back(wind_y, 0), inner_row)
        along_z = face(roll_back(masked, 1), wind_z, roll_back(wind_z, 1), inner_lane)
        for number, value in enumerate(along_x + along_y + along_z):
            faces[number][place] = value
        return next_masked, *following[1:]

    lax.fori_loop(0, total, body, fields(0), unroll=8)


def coefficients(bound):
    theta = (bound + lower_bound) * 0.5
    delta = (bound - lower_bound) * 0.5
    sigma = theta / delta
    rho_one = 1.0 / sigma
    rho_two = 1.0 / (2.0 * sigma - rho_one)
    beta = 2.0 * rho_two / (delta * theta)
    alpha = (1.0 + rho_one * rho_two) / theta + 2.0 * rho_two / delta
    return alpha - beta, beta


def one_step(total, width, layers, state, result, residual, ahead, faces, packed, rate, near, far, rows=0, store=None):
    lanes = state.shape[-1]
    zero = jnp.zeros((width, lanes), jnp.float32)

    def difference(place, values, values_ahead, low_flow, pairs):
        flow_x = pairs[0] * values + pairs[1] * values_ahead
        flow_y = pairs[2] * values + pairs[3] * roll_back(values, 0)
        flow_z = pairs[4] * values + pairs[5] * roll_back(values, 1)
        change = (flow_x - low_flow) + (flow_y - pltpu.roll(flow_y, 1, 0)) + (flow_z - pltpu.roll(flow_z, 1, 1))
        return change, flow_x

    def first_sweep(place, carry):
        values, low_flow = carry
        values_ahead = state[place + 1]
        pairs = []
        for dim in range(3):
            conduct, speed = faces[2 * dim][place], faces[2 * dim + 1][place]
            speed = rate * speed
            pairs.append(conduct + jnp.maximum(speed, 0.0))
            pairs.append(jnp.minimum(speed, 0.0) - conduct)
        for number in range(6):
            ahead[number, place] = pairs[number]
        change, low_flow = difference(place, values, values_ahead, low_flow, pairs)
        spot, layer = place // layers, place % layers
        offset = pl.multiple_of((layers + layer) * width, 8)
        residual[place] = packed[spot, pl.ds(offset, width)] - change
        return values_ahead, low_flow

    def second_sweep(place, carry):
        values, low_flow = carry
        values_ahead = residual[place + 1]
        pairs = [ahead[number, place] for number in range(6)]
        change, low_flow = difference(place, values, values_ahead, low_flow, pairs)
        result[place] = state[place] + (near * values - far * change)
        return values_ahead, low_flow

    lax.fori_loop(0, total, first_sweep, (state[0], zero), unroll=8)
    inner, below, above = pl.ds(LOW, rows), pl.ds(LOW - 1, rows), pl.ds(LOW + 1, rows)

    def inner_sweep(place, carry):
        values, low_flow = carry
        values_ahead = residual[place + 1, inner]
        pairs = [ahead[number, place, inner] for number in range(6)]
        flow_x = pairs[0] * values + pairs[1] * values_ahead
        flow_y = pairs[2] * values + pairs[3] * residual[place, above]
        under_y = ahead[2, place, below] * residual[place, below] + ahead[3, place, below] * values
        flow_z = pairs[4] * values + pairs[5] * roll_back(values, 1)
        change = (flow_x - low_flow) + (flow_y - under_y) + (flow_z - pltpu.roll(flow_z, 1, 1))
        store(place, state[place, inner] + (near * values - far * change))
        return values_ahead, flow_x

    if store is None:
        lax.fori_loop(0, total, second_sweep, (residual[0], zero), unroll=16)
    else:
        lax.fori_loop(0, total, inner_sweep, (residual[0, inner], zero[:rows]), unroll=16)


def bounds_of(packed):
    part = pl.ds(packed.shape[1] - 8, 8)
    bounds = packed[0, part]
    for entry in range(1, packed.shape[0]):
        bounds = jnp.maximum(bounds, packed[entry, part])
    return bounds


def first_kernel(rows, width, layers, info, rates, packed, *refs):
    def store(place, values):
        advanced[place] = values

    faces, (advanced, third, edge_one, edge_two), (state, spare, residual, ahead) = refs[:6], refs[6:10], refs[10:]
    total = state.shape[0] - 1
    zero = jnp.zeros(state.shape[1:], jnp.float32)
    state[total] = zero
    spare[total] = zero
    residual[total] = zero
    for place in range(total):
        state[place] = packed[place // layers, pl.ds(place % layers * width, width)]
    bounds = bounds_of(packed)
    for k in range(FINE):
        near, far = coefficients(bounds[k : k + 1])
        states = (state, spare) if k % 2 == 0 else (spare, state)
        step = (*states, residual, ahead, faces, packed, rates[pl.ds(k, 1)], near, far)
        if k < FINE - 1:
            one_step(total, width, layers, *step)
        else:
            one_step(total, width, layers, *step, rows, store)
        if k == FINE - 2:
            third[...] = states[1][:total, LOW : LOW + rows]
    edge = min(rows, LOW)
    low, high = advanced[:, :edge], advanced[:, rows - edge :]
    even = info[5] % 2 == 0
    edge_one[...] = jnp.where(even, high, low)
    edge_two[...] = jnp.where(even, low, high)


def second_kernel(rows, width, layers, info, rates, packed, passed, halo_one, halo_two, advanced, third, *refs):
    first = info[0] == 0

    def store(place, values):
        out[place // layers, 0, place % layers] = advanced[place]
        out[place // layers, 1, place % layers] = jnp.where(first, third[place], values)

    faces, out, (state, spare, residual, ahead) = refs[:6], refs[6], refs[7:]
    total = state.shape[0] - 1
    zero = jnp.zeros(state.shape[1:], jnp.float32)
    state[total] = zero
    spare[total] = zero
    residual[total] = zero
    swap = info[2] == 1
    below, above = halo_one[...], halo_two[...]
    low = jnp.where(swap, above, below)
    high = jnp.where(swap, below, above)
    state[:total, :LOW] = jnp.where(info[3] == 1, low, 0.0)
    state[:total, LOW : LOW + rows] = passed[...]
    state[:total, LOW + rows : 2 * LOW + rows] = jnp.where(info[4] == 1, high, 0.0)
    if width > 2 * LOW + rows:
        state[:total, 2 * LOW + rows :] = jnp.zeros((total, width - 2 * LOW - rows, state.shape[-1]), jnp.float32)
    bounds = bounds_of(packed)
    for k in range(FINE - 1):
        near, far = coefficients(bounds[k : k + 1])
        states = (state, spare) if k % 2 == 0 else (spare, state)
        step = (*states, residual, ahead, faces, packed, rates[pl.ds(k, 1)], near, far)
        if k < FINE - 2:
            one_step(total, width, layers, *step)
        else:
            one_step(total, width, layers, *step, rows, store)


def unpack_kernel(result, *refs):
    outs, sems = refs[:2], refs[2]
    count, rows = result.shape[0], result.shape[3]
    copies = []
    for number, out in enumerate(outs):
        for spot in range(count):
            target = out.at[0, :, pl.ds(slab_of(spot, count) * rows, rows)]
            copies.append(pltpu.make_async_copy(result.at[spot, number], target, sems.at[number, spot]))
    for copy in copies:
        copy.start()
    for copy in copies:
        copy.wait()


def swapped(array, sizes, partner, flip=0):
    copies, blocks, count = sizes
    pairs = []
    for c in range(copies):
        for t in range(blocks):
            for s in range(count):
                target = partner(t, s)
                if target is not None:
                    pairs.append(((c * blocks + t) * count + s, ((c ^ flip) * blocks + target[0]) * count + target[1]))
    return lax.ppermute(array, AXES, pairs)


def outer_partner(count):
    return lambda t, s: (t, ((s + 1) ^ 1) - 1) if 0 < s < count - 1 else (t ^ 1, s)


def halos(edge_one, edge_two, advanced, sizes, rows, slab):
    copies, blocks, count = sizes
    even = slab % 2 == 0
    below, above = slab > 0, slab < count - 1
    if rows >= LOW and blocks == 2 and count % 2 == 0:
        def partner(t, s):
            own = slab_of(s, count)
            return 1 - t, slab_of(((own + 1) ^ 1) - 1, count) if 0 < own < count - 1 else s

        one = swapped(edge_one, sizes, lambda t, s: (1 - t, s ^ 1))
        two = swapped(edge_two, sizes, partner)
        return one, two, even, below, above

    def shifted(values, by):
        return swapped(
            values, sizes, lambda t, s: (t + 1, s + by) if t + 1 < blocks and 0 <= s + by < count else None
        )

    reach = -(-LOW // rows)
    low = jnp.concatenate([shifted(advanced, by) for by in range(reach, 0, -1)], axis=1)[:, -LOW:]
    high = jnp.concatenate([shifted(advanced, -by) for by in range(1, reach + 1)], axis=1)[:, :LOW]
    return low, high, False, True, True


def shards(sizes, initial, source, diffusion, wind_field, buildings, strength):
    copies, blocks, count = sizes
    layers, depth, lanes = diffusion.shape
    total, rows = layers * count, depth // count
    width = -(-(rows + 2 * LOW) // 8) * 8
    block, place = lax.axis_index("tm"), lax.axis_index("space")
    params = pltpu.CompilerParams(vmem_limit_bytes=48 * 1024 * 1024)

    def struct(*shape):
        return jax.ShapeDtypeStruct(shape, jnp.float32)

    def call(kernel, outs, in_specs, name, *operands, **options):
        return pl.pallas_call(
            kernel,
            out_shape=outs,
            in_specs=in_specs,
            out_specs=[VMEM] * len(outs),
            name=name,
            **{"compiler_params": params, **options},
        )(*operands)

    half = block % 2
    lead = lax.axis_index("copy") % 2
    slab = slab_of(place, count)
    flags = [half, place, place > 0, place < count - 1, lead, slab]
    info = jnp.stack([jnp.asarray(flag).astype(jnp.int32) for flag in flags])
    field = struct(layers, depth, lanes)
    outer = struct(depth, lanes)
    hold = pltpu.VMEM((layers, depth, lanes), jnp.float32)
    anywhere = pl.BlockSpec(memory_space=pltpu.HBM)
    arrays = (initial, source, diffusion, wind_field, buildings, strength)
    shared = [struct(count // 2, layers, width, lanes)] * 2
    masked, winds, state, forcing, edge_one, edge_two, rates, same, across = call(
        functools.partial(load_kernel, rows, width),
        [field, struct(3, layers, depth, lanes), field, field, outer, outer, struct(8, lanes), *shared],
        [SMEM] + [anywhere] * 6,
        "load",
        info,
        *(pltpu.with_memory_space_constraint(array, pltpu.HBM) for array in arrays),
        scratch_shapes=[
            hold,
            hold,
            pltpu.VMEM((layers, depth, lanes), source.dtype),
            pltpu.VMEM((layers, depth, lanes), jnp.int32),
            pltpu.SMEM(strength.shape, jnp.float32),
            pltpu.SemaphoreType.DMA((6,)),
        ],
    )
    across = swapped(across, sizes, lambda t, s: (t, s ^ 1))
    edge_one = swapped(edge_one, sizes, lambda t, s: (t, s ^ 1))
    edge_two = swapped(edge_two, sizes, outer_partner(count))
    edges = jnp.stack([edge_one, edge_two])
    other_edges = swapped(edges, sizes, lambda t, s: (t ^ 1, s))
    (packed,) = call(
        functools.partial(bound_kernel, rows, width),
        [struct(count, 2 * layers * width + 8, lanes)],
        [SMEM] + [VMEM] * 7,
        "bounds",
        info,
        rates,
        edges,
        other_edges,
        masked,
        winds,
        state,
        forcing,
    )
    pieces = jnp.stack([same, across], axis=1)
    parts = [pieces[0]]
    for step in range(1, count // 2):
        parts.append(swapped(pieces[step], sizes, lambda t, s: (t, s ^ (2 * step))))
    *parts, _ = lax.optimization_barrier((*parts, packed))
    packed = lax.all_to_all(packed, "space", 0, 0, tiled=True)
    mine = jnp.concatenate(parts)
    beside = swapped(mine, sizes, lambda t, s: (t, s), 1)
    other = swapped(mine, sizes, lambda t, s: (t ^ 1, s))
    other_beside = swapped(beside, sizes, lambda t, s: (t ^ 1, s))
    faces = call(
        face_kernel,
        [struct(total, width, lanes)] * 6,
        [SMEM] + [VMEM] * 4,
        "faces",
        info,
        mine,
        beside,
        other,
        other_beside,
    )

    edge = min(rows, LOW)
    scratch = [
        pltpu.VMEM((total + 1, width, lanes), jnp.float32),
        pltpu.VMEM((total + 1, width, lanes), jnp.float32),
        pltpu.VMEM((total + 1, width, lanes), jnp.float32),
        pltpu.VMEM((6, total, width, lanes), jnp.float32),
    ]
    advanced, third, edge_one, edge_two = pl.pallas_call(
        functools.partial(first_kernel, rows, width, layers),
        out_shape=[struct(total, rows, lanes)] * 2 + [struct(total, edge, lanes)] * 2,
        in_specs=[SMEM] + [VMEM] * 8,
        out_specs=[VMEM] * 4,
        scratch_shapes=scratch,
        compiler_params=params,
        name="four_steps",
    )(info, rates, packed, *faces)

    if blocks == 2:
        own = swapped(advanced, sizes, lambda t, s: (1 - t, s))
    else:
        own = swapped(advanced, sizes, lambda t, s: (t + 1, s) if t + 1 < blocks else None)
    one, two, swap, below, above = halos(edge_one, edge_two, advanced, sizes, rows, slab)
    flags = [block, place, swap, below, above]
    info = jnp.stack([jnp.asarray(flag).astype(jnp.int32) for flag in flags])
    result = pl.pallas_call(
        functools.partial(second_kernel, rows, width, layers),
        out_shape=struct(count, 2, layers, rows, lanes),
        in_specs=[SMEM] + [VMEM] * 13,
        out_specs=VMEM,
        scratch_shapes=scratch,
        compiler_params=params,
        name="three_steps",
    )(info, rates, packed, own, one, two, advanced, third, *faces)
    result = lax.all_to_all(result, "space", 0, 0, tiled=True)
    if rows % 8:
        result = result.transpose(1, 2, 0, 3, 4).reshape(2, 1, layers, depth, lanes)
        return result[0], result[1]
    return tuple(
        pl.pallas_call(
            unpack_kernel,
            out_shape=[struct(1, layers, depth, lanes)] * 2,
            in_specs=[VMEM],
            out_specs=[pl.BlockSpec(memory_space=pl.ANY)] * 2,
            scratch_shapes=[pltpu.SemaphoreType.DMA((2, count))],
            compiler_params=params,
            name="unpack",
        )(result)
    )


def solution(mesh):
    sizes = tuple(mesh.shape[axis] for axis in AXES)
    in_specs = (
        P(("copy", "tm"), "space", None, None),
        P(("copy", "tm"), "space", None, None),
        P("space", None, None),
        P(None, "space", None, None),
        P("space", None, None),
        P("tm", None),
    )
    out_specs = (P(("copy", "tm"), "space", None, None), P(("copy", "tm"), "space", None, None))
    return jax.shard_map(
        functools.partial(shards, sizes), mesh=mesh, in_specs=in_specs, out_specs=out_specs, check_vma=False
    )
```
